32 devices in a mesh: src: 4 (over y, x), tgt: 8 (over z, core).
Axes of the slice: x: 2, y: 2, z: 4, core: 2. Of those that a mesh axis runs over, the one named last changes fastest.
Arguments:
- source_points: float32 [32, 4096], P(None, 'src'), may hold values from -12 to 12
- target_points: float32 [32, 32768], P('src', 'tgt'), may hold values from -12 to 12
- g_init: float32 [32768], P('tgt'), may hold values from -6 to 6
Outputs:
- source_potential: float32 [4096], P('src')
- target_potential: float32 [32768], P('tgt')
- row_marginal: float32 [4096], P('src')
The draws below stay inside these ranges and needn't reach their ends.
All inputs are finite; a program needn't handle non-finite values.
Results may differ from the reference program's by a relative error of at most 0.0003.
Values sent between devices are 32-bit elements; how exact they have to be, the bound alone decides.
No kernel may reach another device: no remote copies, remote signals or barrier semaphores. Data moves between devices by JAX's collectives and lax.ppermute only.
A program may use at most 64 MiB of HBM per device.

```python
import math
import jax
import jax.numpy as jnp
from jax import lax

DIMS = 32
ITERS = 2
NS = 4096
NT = 32768


def dim_scales():
    return 0.3 / jnp.sqrt(1.0 + jnp.arange(DIMS, dtype=jnp.float32) / 8.0)


def draw_source_points(key, part):
    key = jax.random.fold_in(key, 11)
    first = jax.random.fold_in(key, 0)
    cloud = jnp.clip(jax.random.normal(first, (DIMS, NS), jnp.float32), -4.0, 4.0) * dim_scales()[:, None]
    return cloud


def draw_target_points(key, part):
    key = jax.random.fold_in(key, 23)
    first = jax.random.fold_in(key, 0)
    cloud = jnp.clip(jax.random.normal(first, (DIMS, NT), jnp.float32), -4.0, 4.0) * dim_scales()[:, None]
    return cloud


def draw_g_init(key, part):
    key = jax.random.fold_in(key, 37)
    values = 0.2 * jnp.clip(jax.random.normal(key, (NT,), jnp.float32), -4.0, 4.0)
    return values


def setup_inputs(seed: int = 0) -> dict:
    key_of = jax.random.split(jax.random.key(seed), 4)
    source_points = draw_source_points(jax.random.fold_in(key_of[3], 71), 0)
    target_points = draw_target_points(jax.random.fold_in(key_of[3], 71), 0)
    g_init = draw_g_init(jax.random.fold_in(key_of[3], 71), 0)
    return dict(source_points=source_points, target_points=target_points, g_init=g_init)


epsilon = 0.05


def cost_rows(rows_block, target_points, target_sq):
    rows_sq = jnp.sum(rows_block * rows_block, axis=1)
    cross = jnp.dot(rows_block, target_points, precision=lax.Precision.HIGHEST, preferred_element_type=jnp.float32)
    return rows_sq[:, None] + target_sq[None, :] - 2.0 * cross


def reference(source_points, target_points, g_init):
    width = math.gcd(NS, 512)
    count = NS // width
    blocks = source_points.T.reshape(count, width, DIMS)
    target_sq = jnp.sum(target_points * target_points, axis=0)
    log_nt = math.log(NT)
    log_ns = math.log(NS)
    g_pot = g_init
    f_pot = jnp.zeros((NS,), g_init.dtype)
    for step in range(ITERS):
        def row_lse(rows_block):
            cost = cost_rows(rows_block, target_points, target_sq)
            return jax.nn.logsumexp((g_pot[None, :] - cost) / epsilon, axis=1)

        f_pot = -epsilon * (lax.map(row_lse, blocks).reshape(NS) - log_nt)

        def column_step(carry, packed):
            rows_block, f_block = packed
            cost = cost_rows(rows_block, target_points, target_sq)
            part = jax.nn.logsumexp((f_block[:, None] - cost) / epsilon, axis=0)
            return jnp.logaddexp(carry, part), None

        start = jnp.full((NT,), -jnp.inf, dtype=g_init.dtype)
        total, _ = lax.scan(column_step, start, (blocks, f_pot.reshape(count, width)))
        g_pot = -epsilon * (total - log_ns)

    def marginal_rows(packed):
        rows_block, f_block = packed
        cost = cost_rows(rows_block, target_points, target_sq)
        return jnp.sum(jnp.exp((f_block[:, None] + g_pot[None, :] - cost) / epsilon), axis=1)

    marginal = lax.map(marginal_rows, (blocks, f_pot.reshape(count, width))).reshape(NS) / NT
    return f_pot, g_pot, marginal
```

```python
import functools
import math

import jax
import jax.numpy as jnp
from jax import lax
from jax.experimental import pallas as pl
from jax.experimental.pallas import tpu as pltpu
from jax.sharding import PartitionSpec as P

epsilon = 0.05
KAPPA = math.log2(math.e) / epsilon
LANES = 128
ROW_BLOCK = 256
COL_BLOCK = 512

f32 = jnp.float32
bf16 = jnp.bfloat16
VMEM = pl.BlockSpec(memory_space=pltpu.VMEM)
PARAMS = pltpu.CompilerParams(vmem_limit_bytes=40 * 2**20)


def vmem(shape, dtype=f32):
    return pltpu.VMEM(shape, dtype)


def pin(x):
    return pltpu.with_memory_space_constraint(x, pltpu.VMEM)


def split(x):
    first = x.astype(bf16)
    rest = x - first.astype(f32)
    second = rest.astype(bf16)
    third = (rest - second.astype(f32)).astype(bf16)
    return first, second, third


def to_lanes(x, reduce):
    parts = [
        reduce(x[r : r + LANES].T, axis=0, keepdims=True) for r in range(0, x.shape[0], LANES)
    ]
    return jnp.concatenate(parts, axis=1)


def to_rows(x):
    parts = [
        jnp.broadcast_to(x[:, r : r + LANES], (LANES, LANES)).T
        for r in range(0, x.shape[1], LANES)
    ]
    return jnp.concatenate(parts, axis=0)


def lse2(parts):
    top = functools.reduce(jnp.maximum, parts)
    return top + jnp.log2(sum(jnp.exp2(p - top) for p in parts))


def scores(a_ref, b_ref, row, rows, col, cols):
    return jnp.dot(
        a_ref[pl.ds(row, rows), :], b_ref[:, pl.ds(col, cols)], preferred_element_type=f32
    )


def tiles(width):
    return range(0, width, LANES)


def prepare_rows(n_src, src_ref, a_ref):
    dims, rows = src_ref.shape
    if n_src == 4:
        me, each = lax.axis_index("src"), dims // n_src
        points = jnp.concatenate(
            [src_ref[pl.ds(pl.multiple_of((me ^ k) * each, each), each), :] for k in range(n_src)],
            axis=0,
        )
    else:
        points = src_ref[...]
    s1, s2, s3 = (x.astype(f32) for x in split(points * (2.0 * KAPPA)))
    last = (lax.broadcasted_iota(jnp.int32, (16, rows), 0) < 3).astype(f32)
    a_ref[...] = jnp.concatenate([s1, s1, s2, s1, s3, s2, last], axis=0).T.astype(bf16)


def build(n_blocks, *refs):
    a_ref, g_ref = refs[:2]
    blocks = refs[2 : 2 + n_blocks]
    e_ref, b_ref, rho_ref, m_ref, acc_ref, shift_ref = refs[2 + n_blocks :]
    rows, cols = e_ref.shape
    dims = sum(ref.shape[0] for ref in blocks)
    points = jnp.concatenate([ref[...] for ref in blocks], axis=0)
    t1, t2, t3 = split(points)
    for k, part in enumerate((t1, t2, t1, t3, t1, t2)):
        b_ref[k * dims : (k + 1) * dims, :] = part
    offset = KAPPA * (g_ref[...] - jnp.sum(points * points, axis=0, keepdims=True))
    o1, o2, o3 = (x.astype(f32) for x in split(offset))
    fill = jnp.zeros((13, cols), f32)
    b_ref[6 * dims :, :] = jnp.concatenate([o1, o2, o3, fill], axis=0).astype(bf16)

    def run(columns):
        for row in range(0, rows, ROW_BLOCK):

            def top(i, best):
                s = scores(a_ref, b_ref, row, ROW_BLOCK, pl.multiple_of(i * COL_BLOCK, COL_BLOCK), COL_BLOCK)
                for t in tiles(COL_BLOCK):
                    best = jnp.maximum(best, s[:, t : t + LANES])
                return best

            best = lax.fori_loop(0, columns // COL_BLOCK, top, jnp.full((ROW_BLOCK, LANES), -jnp.inf, f32))
            shift_ref[row : row + ROW_BLOCK, :] = jnp.broadcast_to(
                jnp.max(best, axis=1, keepdims=True), (ROW_BLOCK, LANES)
            )
        acc_ref[...] = jnp.zeros_like(acc_ref)

        def block(i, _):
            col = pl.multiple_of(i * COL_BLOCK, COL_BLOCK)
            for row in range(0, rows, ROW_BLOCK):
                s = scores(a_ref, b_ref, row, ROW_BLOCK, col, COL_BLOCK)
                shift = shift_ref[row : row + ROW_BLOCK, :]
                acc = acc_ref[row : row + ROW_BLOCK, :]
                for t in tiles(COL_BLOCK):
                    e = jnp.exp2(s[:, t : t + LANES] - shift)
                    e_ref[row : row + ROW_BLOCK, pl.ds(pl.multiple_of(col + t, LANES), LANES)] = e
                    acc = acc + e
                acc_ref[row : row + ROW_BLOCK, :] = acc
            return 0

        lax.fori_loop(0, cols // COL_BLOCK, block, 0)
        total = to_lanes(acc_ref[...], jnp.sum)
        shift = to_lanes(shift_ref[...], jnp.max)
        m_ref[...] = shift
        rho_ref[...] = shift + jnp.log2(total)
        return total

    total = run(COL_BLOCK)
    fine = jnp.max(total) < 2.0**100

    @pl.when(jnp.logical_not(fine))
    def _():
        run(cols)


def column_sums(e_ref, u_ref, q_ref):
    rows, cols = e_ref.shape
    width, height = 1024, 64

    for col in range(0, cols, width):

        def body(i, acc):
            row = pl.multiple_of(i * height, height)
            u = u_ref[pl.ds(row, height), :]
            out = []
            for k, t in enumerate(tiles(width)):
                x = e_ref[pl.ds(row, height), col + t : col + t + LANES] * u
                out.append(acc[k] + jnp.sum(x.reshape(height // 8, 8, LANES), axis=0))
            return tuple(out)

        start = tuple(jnp.zeros((8, LANES), f32) for _ in tiles(width))
        acc = lax.fori_loop(0, rows // height, body, start, unroll=4)
        for k, t in enumerate(tiles(width)):
            q_ref[:, col + t : col + t + LANES] = jnp.sum(acc[k], axis=0, keepdims=True)


def row_sums(e_ref, v, v_ref, acc_ref):
    rows, cols = e_ref.shape
    height = 64
    v_ref[...] = v

    def body(i, _):
        row = pl.multiple_of(i * height, height)
        acc = jnp.zeros((height, LANES), f32)
        for t in tiles(cols):
            acc = acc + e_ref[pl.ds(row, height), t : t + LANES] * v_ref[:, t : t + LANES]
        acc_ref[pl.ds(row, height), :] = acc
        return 0

    lax.fori_loop(0, rows // height, body, 0, unroll=4)
    return to_lanes(acc_ref[...], jnp.sum)


def column_pass(n_parts, log_nt, *refs):
    parts = refs[:n_parts]
    m_ref, e_ref, a_ref, b_ref, lam_ref, f_ref, u_ref, q_ref = refs[n_parts:]
    rows, cols = e_ref.shape
    pot = log_nt - lse2([ref[...] for ref in parts])
    f_ref[...] = pot
    power = pot + m_ref[...]
    u = jnp.exp2(power)
    u_ref[...] = to_rows(u)
    column_sums(e_ref, u_ref, q_ref)
    q = q_ref[...]
    lam_ref[...] = jnp.log2(q)
    least = jnp.maximum(jnp.sum(u) * 2.0**-106, 2.0**-96)
    fine = (jnp.min(power) > -100.0) & (jnp.min(q) >= least) & (jnp.max(q) < 2.0**120)

    @pl.when(jnp.logical_not(fine))
    def _():
        u_ref[...] = to_rows(pot)

        def block(c, _):
            col = pl.multiple_of(c * COL_BLOCK, COL_BLOCK)

            def shifted(i):
                row = pl.multiple_of(i * LANES, LANES)
                s = scores(a_ref, b_ref, row, LANES, col, COL_BLOCK)
                return s + jnp.concatenate([u_ref[pl.ds(row, LANES), :]] * (COL_BLOCK // LANES), axis=1)

            top = lax.fori_loop(
                0,
                rows // LANES,
                lambda i, best: jnp.maximum(best, jnp.max(shifted(i), axis=0, keepdims=True)),
                jnp.full((1, COL_BLOCK), -jnp.inf, f32),
            )
            total = lax.fori_loop(
                0,
                rows // LANES,
                lambda i, acc: acc + jnp.sum(jnp.exp2(shifted(i) - top), axis=0, keepdims=True),
                jnp.zeros((1, COL_BLOCK), f32),
            )
            lam_ref[:, pl.ds(col, COL_BLOCK)] = top + jnp.log2(total)
            return 0

        lax.fori_loop(0, cols // COL_BLOCK, block, 0)


def row_log_sums(parts, log_ns, m_ref, e_ref, a_ref, b_ref, rho_ref, v_ref, acc_ref):
    rows, cols = e_ref.shape
    change = log_ns - lse2([ref[...] for ref in parts])
    v = jnp.exp2(change)
    r = row_sums(e_ref, v, v_ref, acc_ref)
    rho_ref[...] = m_ref[...] + jnp.log2(r)
    least = jnp.maximum(jnp.sum(v) * 2.0**-106, 2.0**-94)
    fine = (jnp.min(change) > -100.0) & (jnp.min(r) >= least) & (jnp.max(r) < 2.0**120)

    @pl.when(jnp.logical_not(fine))
    def _():
        v_ref[...] = change

        def block(i, _):
            row = pl.multiple_of(i * LANES, LANES)

            def shifted(c):
                col = pl.multiple_of(c * COL_BLOCK, COL_BLOCK)
                return scores(a_ref, b_ref, row, LANES, col, COL_BLOCK) + v_ref[:, pl.ds(col, COL_BLOCK)]

            top = lax.fori_loop(
                0,
                cols // COL_BLOCK,
                lambda c, best: jnp.maximum(best, jnp.max(shifted(c), axis=1, keepdims=True)),
                jnp.full((LANES, 1), -jnp.inf, f32),
            )
            total = lax.fori_loop(
                0,
                cols // COL_BLOCK,
                lambda c, acc: acc + jnp.sum(jnp.exp2(shifted(c) - top), axis=1, keepdims=True),
                jnp.zeros((LANES, 1), f32),
            )
            value = jnp.broadcast_to(top + jnp.log2(total), (LANES, LANES))
            rho_ref[:, pl.ds(row, LANES)] = jnp.max(value.T, axis=0, keepdims=True)
            return 0

        lax.fori_loop(0, rows // LANES, block, 0)

    return change


def row_pass(n_parts, log_ns, *refs):
    parts = refs[:n_parts]
    m_ref, e_ref, a_ref, b_ref, rho_ref, v_ref, acc_ref = refs[n_parts:]
    row_log_sums(parts, log_ns, m_ref, e_ref, a_ref, b_ref, rho_ref, v_ref, acc_ref)


def marginal_pass(n_parts, log_ns, *refs):
    parts = refs[:n_parts]
    m_ref, e_ref, a_ref, b_ref, f_ref, g_ref, sum_ref, new_g_ref, rho_ref, v_ref, acc_ref = refs[n_parts:]
    change = row_log_sums(parts, log_ns, m_ref, e_ref, a_ref, b_ref, rho_ref, v_ref, acc_ref)
    new_g_ref[...] = g_ref[...] + change * (1.0 / KAPPA)
    sum_ref[...] = jnp.exp2(f_ref[...] + rho_ref[...])


def others(x, axis, size, steps):
    return [lax.ppermute(x, axis, [(i, i ^ k) for i in range(size)]) for k in steps]


def pool_src(x):
    size = lax.axis_size("src")
    if size == 4:
        return [x] + others(x, "src", size, (1, 2, 3))
    every = lax.all_gather(x, "src", axis=0)
    return [every[k] for k in range(size)]


def pool_tgt(x, join):
    size = lax.axis_size("tgt")
    if size == 8:
        x = join([x] + others(x, "tgt", size, (1,)))
        return [x] + others(x, "tgt", size, (2, 4, 6))
    every = lax.all_gather(x, "tgt", axis=0)
    return [every[k] for k in range(size)]


def body(source_points, target_points, g_init):
    dims, rows = source_points.shape
    cols = target_points.shape[1]
    n_src, n_tgt = lax.axis_size("src"), lax.axis_size("tgt")
    log_nt, log_ns = math.log2(cols * n_tgt), math.log2(rows * n_src)
    depth = 6 * dims + 16
    row, col, square = vmem((1, rows)), vmem((1, cols)), vmem((rows, LANES))

    if n_src == 4:
        blocks = pool_src(target_points)
    else:
        blocks = [lax.all_gather(target_points, "src", axis=0, tiled=True)]
    a = pl.pallas_call(
        functools.partial(prepare_rows, n_src),
        out_shape=vmem((rows, depth), bf16),
        in_specs=[VMEM],
        out_specs=VMEM,
        compiler_params=PARAMS,
    )(source_points)
    g = g_init.reshape(1, cols)
    e, b, rho, m = pl.pallas_call(
        functools.partial(build, len(blocks)),
        out_shape=(vmem((rows, cols)), vmem((depth, cols), bf16), row, row),
        in_specs=[VMEM] * (2 + len(blocks)),
        out_specs=(VMEM,) * 4,
        scratch_shapes=[square, square],
        compiler_params=PARAMS,
    )(pin(a), g, *blocks)
    a, e, b, m = pin(a), pin(e), pin(b), pin(m)

    def columns(rho):
        parts = pool_tgt(rho, lse2)
        return pl.pallas_call(
            functools.partial(column_pass, len(parts), log_nt),
            out_shape=(col, row),
            in_specs=[VMEM] * (len(parts) + 4),
            out_specs=(VMEM, VMEM),
            scratch_shapes=[square, col],
            compiler_params=PARAMS,
        )(*parts, m, e, a, b)

    lam, _ = columns(rho)
    parts = pool_src(lam)
    rho = pl.pallas_call(
        functools.partial(row_pass, len(parts), log_ns),
        out_shape=row,
        in_specs=[VMEM] * (len(parts) + 4),
        out_specs=VMEM,
        scratch_shapes=[col, square],
        compiler_params=PARAMS,
    )(*parts, m, e, a, b)
    lam, f = columns(rho)
    parts = pool_src(lam)
    total, g_pot = pl.pallas_call(
        functools.partial(marginal_pass, len(parts), log_ns),
        out_shape=(row, jax.ShapeDtypeStruct((1, cols), f32)),
        in_specs=[VMEM] * (len(parts) + 6),
        out_specs=(VMEM, VMEM),
        scratch_shapes=[row, col, square],
        compiler_params=PARAMS,
    )(*parts, m, e, a, b, f, g)
    marginal = sum(pool_tgt(total, sum)) * (1.0 / (cols * n_tgt))
    f_pot = jnp.sum(source_points * source_points, axis=0) + f.reshape(rows) * (1.0 / KAPPA)
    return f_pot, g_pot.reshape(cols), marginal.reshape(rows)


def solution(mesh):
    in_specs = (P(None, "src"), P("src", "tgt"), P("tgt"))
    out_specs = (P("src"), P("tgt"), P("src"))
    return jax.shard_map(body, mesh=mesh, in_specs=in_specs, out_specs=out_specs, check_vma=False)
```

```python
import functools
import math

import jax
import jax.numpy as jnp
from jax import lax
from jax.experimental import pallas as pl
from jax.experimental.pallas import tpu as pltpu
from jax.sharding import PartitionSpec as P

epsilon = 0.05
KAPPA = math.log2(math.e) / epsilon
LANES = 128
ROW_BLOCK = 256
COL_BLOCK = 512

f32 = jnp.float32
bf16 = jnp.bfloat16
VMEM = pl.BlockSpec(memory_space=pltpu.VMEM)
PARAMS = pltpu.CompilerParams(vmem_limit_bytes=16 * 2**20)


def vmem(shape, dtype=f32):
    return pltpu.VMEM(shape, dtype)


def pin(x):
    return pltpu.with_memory_space_constraint(x, pltpu.VMEM)


def split(x):
    first = x.astype(bf16)
    rest = x - first.astype(f32)
    second = rest.astype(bf16)
    third = (rest - second.astype(f32)).astype(bf16)
    return first, second, third


def to_lanes(x, reduce):
    parts = [
        reduce(x[r : r + LANES].T, axis=0, keepdims=True) for r in range(0, x.shape[0], LANES)
    ]
    return jnp.concatenate(parts, axis=1)


def to_rows(x):
    parts = [
        jnp.broadcast_to(x[:, r : r + LANES], (LANES, LANES)).T
        for r in range(0, x.shape[1], LANES)
    ]
    return jnp.concatenate(parts, axis=0)


def lse2(parts):
    top = functools.reduce(jnp.maximum, parts)
    return top + jnp.log2(sum(jnp.exp2(p - top) for p in parts))


def scores(a_ref, b_ref, row, rows, col, cols):
    return jnp.dot(
        a_ref[pl.ds(row, rows), :], b_ref[:, pl.ds(col, cols)], preferred_element_type=f32
    )


def tiles(width):
    return range(0, width, LANES)


def prepare_rows(n_src, src_ref, a_ref):
    dims, rows = src_ref.shape
    if n_src == 4:
        me, each = lax.axis_index("src"), dims // n_src
        points = jnp.concatenate(
            [src_ref[pl.ds(pl.multiple_of((me ^ k) * each, each), each), :] for k in range(n_src)],
            axis=0,
        )
    else:
        points = src_ref[...]
    s1, s2, s3 = (x.astype(f32) for x in split(points * (2.0 * KAPPA)))
    last = (lax.broadcasted_iota(jnp.int32, (16, rows), 0) < 3).astype(f32)
    a_ref[...] = jnp.concatenate([s1, s1, s2, s1, s3, s2, last], axis=0).T.astype(bf16)


def build(n_blocks, *refs):
    a_ref, g_ref = refs[:2]
    blocks = refs[2 : 2 + n_blocks]
    e_ref, b_ref, rho_ref, m_ref, acc_ref, shift_ref = refs[2 + n_blocks :]
    rows, cols = e_ref.shape
    dims = sum(ref.shape[0] for ref in blocks)
    points = jnp.concatenate([ref[...] for ref in blocks], axis=0)
    t1, t2, t3 = split(points)
    for k, part in enumerate((t1, t2, t1, t3, t1, t2)):
        b_ref[k * dims : (k + 1) * dims, :] = part
    offset = KAPPA * (g_ref[...] - jnp.sum(points * points, axis=0, keepdims=True))
    o1, o2, o3 = (x.astype(f32) for x in split(offset))
    fill = jnp.zeros((13, cols), f32)
    b_ref[6 * dims :, :] = jnp.concatenate([o1, o2, o3, fill], axis=0).astype(bf16)

    def run(columns):
        for row in range(0, rows, ROW_BLOCK):

            def top(i, best):
                s = scores(a_ref, b_ref, row, ROW_BLOCK, pl.multiple_of(i * COL_BLOCK, COL_BLOCK), COL_BLOCK)
                for t in tiles(COL_BLOCK):
                    best = jnp.maximum(best, s[:, t : t + LANES])
                return best

            best = lax.fori_loop(0, columns // COL_BLOCK, top, jnp.full((ROW_BLOCK, LANES), -jnp.inf, f32))
            shift_ref[row : row + ROW_BLOCK, :] = jnp.broadcast_to(
                jnp.max(best, axis=1, keepdims=True), (ROW_BLOCK, LANES)
            )
        acc_ref[...] = jnp.zeros_like(acc_ref)

        def block(i, _):
            col = pl.multiple_of(i * COL_BLOCK, COL_BLOCK)
            for row in range(0, rows, ROW_BLOCK):
                s = scores(a_ref, b_ref, row, ROW_BLOCK, col, COL_BLOCK)
                shift = shift_ref[row : row + ROW_BLOCK, :]
                acc = acc_ref[row : row + ROW_BLOCK, :]
                for t in tiles(COL_BLOCK):
                    e = jnp.exp2(s[:, t : t + LANES] - shift)
                    e_ref[row : row + ROW_BLOCK, pl.ds(pl.multiple_of(col + t, LANES), LANES)] = e
                    acc = acc + e
                acc_ref[row : row + ROW_BLOCK, :] = acc
            return 0

        lax.fori_loop(0, cols // COL_BLOCK, block, 0)
        total = to_lanes(acc_ref[...], jnp.sum)
        shift = to_lanes(shift_ref[...], jnp.max)
        m_ref[...] = shift
        rho_ref[...] = shift + jnp.log2(total)
        return total

    total = run(COL_BLOCK)
    fine = jnp.max(total) < 2.0**100

    @pl.when(jnp.logical_not(fine))
    def _():
        run(cols)


def column_sums(e_ref, u_ref, q_ref):
    rows, cols = e_ref.shape
    width, height = 1024, 64

    for col in range(0, cols, width):

        def body(i, acc):
            row = pl.multiple_of(i * height, height)
            u = u_ref[pl.ds(row, height), :]
            out = []
            for k, t in enumerate(tiles(width)):
                x = e_ref[pl.ds(row, height), col + t : col + t + LANES] * u
                out.append(acc[k] + jnp.sum(x.reshape(height // 8, 8, LANES), axis=0))
            return tuple(out)

        start = tuple(jnp.zeros((8, LANES), f32) for _ in tiles(width))
        acc = lax.fori_loop(0, rows // height, body, start, unroll=4)
        for k, t in enumerate(tiles(width)):
            q_ref[:, col + t : col + t + LANES] = jnp.sum(acc[k], axis=0, keepdims=True)


def row_sums(e_ref, v, v_ref, acc_ref):
    rows, cols = e_ref.shape
    height = 64
    v_ref[...] = v

    def body(i, _):
        row = pl.multiple_of(i * height, height)
        acc = jnp.zeros((height, LANES), f32)
        for t in tiles(cols):
            acc = acc + e_ref[pl.ds(row, height), t : t + LANES] * v_ref[:, t : t + LANES]
        acc_ref[pl.ds(row, height), :] = acc
        return 0

    lax.fori_loop(0, rows // height, body, 0, unroll=4)
    return to_lanes(acc_ref[...], jnp.sum)


def column_pass(n_parts, log_nt, *refs):
    parts = refs[:n_parts]
    m_ref, e_ref, a_ref, b_ref, lam_ref, f_ref, u_ref, q_ref = refs[n_parts:]
    rows, cols = e_ref.shape
    pot = log_nt - lse2([ref[...] for ref in parts])
    f_ref[...] = pot
    power = pot + m_ref[...]
    u = jnp.exp2(power)
    u_ref[...] = to_rows(u)
    column_sums(e_ref, u_ref, q_ref)
    q = q_ref[...]
    lam_ref[...] = jnp.log2(q)
    least = jnp.maximum(jnp.sum(u) * 2.0**-106, 2.0**-96)
    fine = (jnp.min(power) > -100.0) & (jnp.min(q) >= least) & (jnp.max(q) < 2.0**120)

    @pl.when(jnp.logical_not(fine))
    def _():
        u_ref[...] = to_rows(pot)

        def block(c, _):
            col = pl.multiple_of(c * COL_BLOCK, COL_BLOCK)

            def shifted(i):
                row = pl.multiple_of(i * LANES, LANES)
                s = scores(a_ref, b_ref, row, LANES, col, COL_BLOCK)
                return s + jnp.concatenate([u_ref[pl.ds(row, LANES), :]] * (COL_BLOCK // LANES), axis=1)

            top = lax.fori_loop(
                0,
                rows // LANES,
                lambda i, best: jnp.maximum(best, jnp.max(shifted(i), axis=0, keepdims=True)),
                jnp.full((1, COL_BLOCK), -jnp.inf, f32),
            )
            total = lax.fori_loop(
                0,
                rows // LANES,
                lambda i, acc: acc + jnp.sum(jnp.exp2(shifted(i) - top), axis=0, keepdims=True),
                jnp.zeros((1, COL_BLOCK), f32),
            )
            lam_ref[:, pl.ds(col, COL_BLOCK)] = top + jnp.log2(total)
            return 0

        lax.fori_loop(0, cols // COL_BLOCK, block, 0)


def row_log_sums(parts, log_ns, m_ref, e_ref, a_ref, b_ref, rho_ref, v_ref, acc_ref):
    rows, cols = e_ref.shape
    change = log_ns - lse2([ref[...] for ref in parts])
    v = jnp.exp2(change)
    r = row_sums(e_ref, v, v_ref, acc_ref)
    rho_ref[...] = m_ref[...] + jnp.log2(r)
    least = jnp.maximum(jnp.sum(v) * 2.0**-106, 2.0**-94)
    fine = (jnp.min(change) > -100.0) & (jnp.min(r) >= least) & (jnp.max(r) < 2.0**120)

    @pl.when(jnp.logical_not(fine))
    def _():
        v_ref[...] = change

        def block(i, _):
            row = pl.multiple_of(i * LANES, LANES)

            def shifted(c):
                col = pl.multiple_of(c * COL_BLOCK, COL_BLOCK)
                return scores(a_ref, b_ref, row, LANES, col, COL_BLOCK) + v_ref[:, pl.ds(col, COL_BLOCK)]

            top = lax.fori_loop(
                0,
                cols // COL_BLOCK,
                lambda c, best: jnp.maximum(best, jnp.max(shifted(c), axis=1, keepdims=True)),
                jnp.full((LANES, 1), -jnp.inf, f32),
            )
            total = lax.fori_loop(
                0,
                cols // COL_BLOCK,
                lambda c, acc: acc + jnp.sum(jnp.exp2(shifted(c) - top), axis=1, keepdims=True),
                jnp.zeros((LANES, 1), f32),
            )
            value = jnp.broadcast_to(top + jnp.log2(total), (LANES, LANES))
            rho_ref[:, pl.ds(row, LANES)] = jnp.max(value.T, axis=0, keepdims=True)
            return 0

        lax.fori_loop(0, rows // LANES, block, 0)

    return change


def row_pass(n_parts, log_ns, *refs):
    parts = refs[:n_parts]
    m_ref, e_ref, a_ref, b_ref, rho_ref, v_ref, acc_ref = refs[n_parts:]
    row_log_sums(parts, log_ns, m_ref, e_ref, a_ref, b_ref, rho_ref, v_ref, acc_ref)


def marginal_pass(n_parts, log_ns, *refs):
    parts = refs[:n_parts]
    m_ref, e_ref, a_ref, b_ref, f_ref, g_ref, sum_ref, new_g_ref, rho_ref, v_ref, acc_ref = refs[n_parts:]
    change = row_log_sums(parts, log_ns, m_ref, e_ref, a_ref, b_ref, rho_ref, v_ref, acc_ref)
    new_g_ref[...] = g_ref[...] + change * (1.0 / KAPPA)
    sum_ref[...] = jnp.exp2(f_ref[...] + rho_ref[...])


def others(x, axis, size, steps):
    return [lax.ppermute(x, axis, [(i, i ^ k) for i in range(size)]) for k in steps]


def pool_src(x):
    size = lax.axis_size("src")
    if size == 4:
        return [x] + others(x, "src", size, (1, 2, 3))
    every = lax.all_gather(x, "src", axis=0)
    return [every[k] for k in range(size)]


def pool_tgt(x, join):
    size = lax.axis_size("tgt")
    if size == 8:
        x = join([x] + others(x, "tgt", size, (1,)))
        return [x] + others(x, "tgt", size, (2, 4, 6))
    every = lax.all_gather(x, "tgt", axis=0)
    return [every[k] for k in range(size)]


def body(source_points, target_points, g_init):
    dims, rows = source_points.shape
    cols = target_points.shape[1]
    n_src, n_tgt = lax.axis_size("src"), lax.axis_size("tgt")
    log_nt, log_ns = math.log2(cols * n_tgt), math.log2(rows * n_src)
    depth = 6 * dims + 16
    row, col, square = vmem((1, rows)), vmem((1, cols)), vmem((rows, LANES))

    if n_src == 4:
        blocks = pool_src(target_points)
    else:
        blocks = [lax.all_gather(target_points, "src", axis=0, tiled=True)]
    a = pl.pallas_call(
        functools.partial(prepare_rows, n_src),
        out_shape=vmem((rows, depth), bf16),
        in_specs=[VMEM],
        out_specs=VMEM,
        compiler_params=PARAMS,
    )(source_points)
    g = g_init.reshape(1, cols)
    e, b, rho, m = pl.pallas_call(
        functools.partial(build, len(blocks)),
        out_shape=(vmem((rows, cols)), vmem((depth, cols), bf16), row, row),
        in_specs=[VMEM] * (2 + len(blocks)),
        out_specs=(VMEM,) * 4,
        scratch_shapes=[square, square],
        compiler_params=PARAMS,
    )(pin(a), g, *map(pin, blocks))
    a, e, b, m = pin(a), pin(e), pin(b), pin(m)

    def columns(rho):
        parts = pool_tgt(rho, lse2)
        return pl.pallas_call(
            functools.partial(column_pass, len(parts), log_nt),
            out_shape=(col, row),
            in_specs=[VMEM] * (len(parts) + 4),
            out_specs=(VMEM, VMEM),
            scratch_shapes=[square, col],
            compiler_params=PARAMS,
        )(*map(pin, parts), m, e, a, b)

    lam, _ = columns(rho)
    parts = pool_src(lam)
    rho = pl.pallas_call(
        functools.partial(row_pass, len(parts), log_ns),
        out_shape=row,
        in_specs=[VMEM] * (len(parts) + 4),
        out_specs=VMEM,
        scratch_shapes=[col, square],
        compiler_params=PARAMS,
    )(*map(pin, parts), m, e, a, b)
    lam, f = columns(rho)
    parts = pool_src(lam)
    total, g_pot = pl.pallas_call(
        functools.partial(marginal_pass, len(parts), log_ns),
        out_shape=(row, jax.ShapeDtypeStruct((1, cols), f32)),
        in_specs=[VMEM] * (len(parts) + 6),
        out_specs=(VMEM, VMEM),
        scratch_shapes=[row, col, square],
        compiler_params=PARAMS,
    )(*map(pin, parts), m, e, a, b, pin(f), g)
    marginal = sum(pool_tgt(total, sum)) * (1.0 / (cols * n_tgt))
    f_pot = jnp.sum(source_points * source_points, axis=0) + f.reshape(rows) * (1.0 / KAPPA)
    return f_pot, g_pot.reshape(cols), marginal.reshape(rows)


def solution(mesh):
    in_specs = (P(None, "src"), P("src", "tgt"), P("tgt"))
    out_specs = (P("src"), P("tgt"), P("src"))
    return jax.shard_map(body, mesh=mesh, in_specs=in_specs, out_specs=out_specs, check_vma=False)
```

```python
import functools
import math

import jax
import jax.numpy as jnp
from jax import lax
from jax.experimental import pallas as pl
from jax.experimental.pallas import tpu as pltpu
from jax.sharding import PartitionSpec as P

epsilon = 0.05
KAPPA = math.log2(math.e) / epsilon
LANES = 128
ROW_BLOCK = 512
COL_BLOCK = 256

f32 = jnp.float32
bf16 = jnp.bfloat16
VMEM = pl.BlockSpec(memory_space=pltpu.VMEM)
PARAMS = pltpu.CompilerParams(vmem_limit_bytes=16 * 2**20)


def vmem(shape, dtype=f32):
    return pltpu.VMEM(shape, dtype)


def pin(x):
    return pltpu.with_memory_space_constraint(x, pltpu.VMEM)


def split(x):
    first = x.astype(bf16)
    rest = x - first.astype(f32)
    second = rest.astype(bf16)
    third = (rest - second.astype(f32)).astype(bf16)
    return first, second, third


def to_lanes(x, reduce):
    parts = [
        reduce(x[r : r + LANES].T, axis=0, keepdims=True) for r in range(0, x.shape[0], LANES)
    ]
    return jnp.concatenate(parts, axis=1)


def to_rows(x):
    parts = [
        jnp.broadcast_to(x[:, r : r + LANES], (LANES, LANES)).T
        for r in range(0, x.shape[1], LANES)
    ]
    return jnp.concatenate(parts, axis=0)


def lse2(parts):
    top = functools.reduce(jnp.maximum, parts)
    return top + jnp.log2(sum(jnp.exp2(p - top) for p in parts))


def scores(a_ref, b_ref, row, rows, col, cols):
    return jnp.dot(
        a_ref[pl.ds(row, rows), :], b_ref[:, pl.ds(col, cols)], preferred_element_type=f32
    )


def tiles(width):
    return range(0, width, LANES)


def prepare(n_src, src_ref, t_ref, g_ref, a_ref, own_ref, start_ref):
    own_ref[...] = t_ref[...]
    start_ref[...] = g_ref[...]
    dims, rows = src_ref.shape
    if n_src == 4:
        me, each = lax.axis_index("src"), dims // n_src
        points = jnp.concatenate(
            [src_ref[pl.ds(pl.multiple_of((me ^ k) * each, each), each), :] for k in range(n_src)],
            axis=0,
        )
    else:
        points = src_ref[...]
    s1, s2, s3 = (x.astype(f32) for x in split(points * (2.0 * KAPPA)))
    last = (lax.broadcasted_iota(jnp.int32, (16, rows), 0) < 3).astype(f32)
    a_ref[...] = jnp.concatenate([s1, s1, s2, s1, s3, s2, last], axis=0).T.astype(bf16)


def build(n_blocks, *refs):
    a_ref, g_ref = refs[:2]
    blocks = refs[2 : 2 + n_blocks]
    e_ref, b_ref, rho_ref, m_ref, acc_ref, shift_ref = refs[2 + n_blocks :]
    rows, cols = e_ref.shape
    dims = sum(ref.shape[0] for ref in blocks)
    points = jnp.concatenate([ref[...] for ref in blocks], axis=0)
    t1, t2, t3 = split(points)
    for k, part in enumerate((t1, t2, t1, t3, t1, t2)):
        b_ref[k * dims : (k + 1) * dims, :] = part
    offset = KAPPA * (g_ref[...] - jnp.sum(points * points, axis=0, keepdims=True))
    o1, o2, o3 = (x.astype(f32) for x in split(offset))
    fill = jnp.zeros((13, cols), f32)
    b_ref[6 * dims :, :] = jnp.concatenate([o1, o2, o3, fill], axis=0).astype(bf16)

    def block(i, wide):
        row = pl.multiple_of(i * ROW_BLOCK, ROW_BLOCK)
        here = pl.ds(row, ROW_BLOCK)

        def top(col):
            s = scores(a_ref, b_ref, row, ROW_BLOCK, col, COL_BLOCK)
            return s, functools.reduce(jnp.maximum, [s[:, t : t + LANES] for t in tiles(COL_BLOCK)])

        def spread(best):
            return jnp.broadcast_to(jnp.max(best, axis=1, keepdims=True), best.shape)

        if wide:
            best = lax.fori_loop(
                1,
                cols // COL_BLOCK,
                lambda c, best: jnp.maximum(best, top(pl.multiple_of(c * COL_BLOCK, COL_BLOCK))[1]),
                top(0)[1],
            )
            shift_ref[here, :] = spread(best)
        for col in range(0, cols, COL_BLOCK):
            if col == 0 and not wide:
                s, best = top(0)
                shift = spread(best)
                shift_ref[here, :] = shift
            else:
                s = scores(a_ref, b_ref, row, ROW_BLOCK, col, COL_BLOCK)
                shift = shift_ref[here, :]
            acc = acc_ref[here, :] if col else 0.0
            for t in tiles(COL_BLOCK):
                e = jnp.exp2(s[:, t : t + LANES] - shift)
                e_ref[here, col + t : col + t + LANES] = e
                acc = acc + e
            acc_ref[here, :] = acc

    def run(wide):
        lax.fori_loop(0, rows // ROW_BLOCK, lambda i, _: block(i, wide), None)
        total = to_lanes(acc_ref[...], jnp.sum)
        shift = to_lanes(shift_ref[...], jnp.max)
        m_ref[...] = shift
        rho_ref[...] = shift + jnp.log2(total)
        return total

    total = run(False)
    fine = jnp.max(total) < 2.0**100

    @pl.when(jnp.logical_not(fine))
    def _():
        run(True)


def column_sums(e_ref, u_ref, q_ref):
    rows, cols = e_ref.shape
    width, height = 1024, 64

    for col in range(0, cols, width):

        def body(i, acc):
            row = pl.multiple_of(i * height, height)
            u = u_ref[pl.ds(row, height), :]
            out = []
            for k, t in enumerate(tiles(width)):
                x = e_ref[pl.ds(row, height), col + t : col + t + LANES] * u
                out.append(acc[k] + jnp.sum(x.reshape(height // 8, 8, LANES), axis=0))
            return tuple(out)

        start = tuple(jnp.zeros((8, LANES), f32) for _ in tiles(width))
        acc = lax.fori_loop(0, rows // height, body, start, unroll=4)
        for k, t in enumerate(tiles(width)):
            q_ref[:, col + t : col + t + LANES] = jnp.sum(acc[k], axis=0, keepdims=True)


def row_sums(e_ref, v, v_ref, acc_ref):
    rows, cols = e_ref.shape
    height = 64
    v_ref[...] = v

    def body(i, _):
        row = pl.multiple_of(i * height, height)
        acc = jnp.zeros((height, LANES), f32)
        for t in tiles(cols):
            acc = acc + e_ref[pl.ds(row, height), t : t + LANES] * v_ref[:, t : t + LANES]
        acc_ref[pl.ds(row, height), :] = acc
        return 0

    lax.fori_loop(0, rows // height, body, 0, unroll=4)
    return to_lanes(acc_ref[...], jnp.sum)


def column_pass(n_parts, log_nt, *refs):
    parts = refs[:n_parts]
    m_ref, e_ref, a_ref, b_ref, lam_ref, *f_ref, u_ref, q_ref = refs[n_parts:]
    rows, cols = e_ref.shape
    pot = log_nt - lse2([ref[...] for ref in parts])
    for ref in f_ref:
        ref[...] = pot
    power = pot + m_ref[...]
    u = jnp.exp2(power)
    u_ref[...] = to_rows(u)
    column_sums(e_ref, u_ref, q_ref)
    q = q_ref[...]
    lam_ref[...] = jnp.log2(q)
    least = jnp.maximum(jnp.sum(u) * 2.0**-106, 2.0**-96)
    fine = (jnp.min(power) > -100.0) & (jnp.min(q) >= least) & (jnp.max(q) < 2.0**120)

    @pl.when(jnp.logical_not(fine))
    def _():
        u_ref[...] = to_rows(pot)

        def block(c, _):
            col = pl.multiple_of(c * COL_BLOCK, COL_BLOCK)

            def shifted(i):
                row = pl.multiple_of(i * LANES, LANES)
                s = scores(a_ref, b_ref, row, LANES, col, COL_BLOCK)
                return s + jnp.concatenate([u_ref[pl.ds(row, LANES), :]] * (COL_BLOCK // LANES), axis=1)

            top = lax.fori_loop(
                0,
                rows // LANES,
                lambda i, best: jnp.maximum(best, jnp.max(shifted(i), axis=0, keepdims=True)),
                jnp.full((1, COL_BLOCK), -jnp.inf, f32),
            )
            total = lax.fori_loop(
                0,
                rows // LANES,
                lambda i, acc: acc + jnp.sum(jnp.exp2(shifted(i) - top), axis=0, keepdims=True),
                jnp.zeros((1, COL_BLOCK), f32),
            )
            lam_ref[:, pl.ds(col, COL_BLOCK)] = top + jnp.log2(total)
            return 0

        lax.fori_loop(0, cols // COL_BLOCK, block, 0)


def row_log_sums(parts, log_ns, m_ref, e_ref, a_ref, b_ref, rho_ref, v_ref, acc_ref):
    rows, cols = e_ref.shape
    change = log_ns - lse2([ref[...] for ref in parts])
    v = jnp.exp2(change)
    r = row_sums(e_ref, v, v_ref, acc_ref)
    rho_ref[...] = m_ref[...] + jnp.log2(r)
    least = jnp.maximum(jnp.sum(v) * 2.0**-106, 2.0**-94)
    fine = (jnp.min(change) > -100.0) & (jnp.min(r) >= least) & (jnp.max(r) < 2.0**120)

    @pl.when(jnp.logical_not(fine))
    def _():
        v_ref[...] = change

        def block(i, _):
            row = pl.multiple_of(i * LANES, LANES)

            def shifted(c):
                col = pl.multiple_of(c * COL_BLOCK, COL_BLOCK)
                return scores(a_ref, b_ref, row, LANES, col, COL_BLOCK) + v_ref[:, pl.ds(col, COL_BLOCK)]

            top = lax.fori_loop(
                0,
                cols // COL_BLOCK,
                lambda c, best: jnp.maximum(best, jnp.max(shifted(c), axis=1, keepdims=True)),
                jnp.full((LANES, 1), -jnp.inf, f32),
            )
            total = lax.fori_loop(
                0,
                cols // COL_BLOCK,
                lambda c, acc: acc + jnp.sum(jnp.exp2(shifted(c) - top), axis=1, keepdims=True),
                jnp.zeros((LANES, 1), f32),
            )
            value = jnp.broadcast_to(top + jnp.log2(total), (LANES, LANES))
            rho_ref[:, pl.ds(row, LANES)] = jnp.max(value.T, axis=0, keepdims=True)
            return 0

        lax.fori_loop(0, rows // LANES, block, 0)

    return change


def row_pass(n_parts, log_ns, *refs):
    parts = refs[:n_parts]
    m_ref, e_ref, a_ref, b_ref, rho_ref, v_ref, acc_ref = refs[n_parts:]
    row_log_sums(parts, log_ns, m_ref, e_ref, a_ref, b_ref, rho_ref, v_ref, acc_ref)


def marginal_pass(n_parts, log_ns, *refs):
    parts = refs[:n_parts]
    m_ref, e_ref, a_ref, b_ref, f_ref, g_ref, sum_ref, new_g_ref, rho_ref, v_ref, acc_ref = refs[n_parts:]
    change = row_log_sums(parts, log_ns, m_ref, e_ref, a_ref, b_ref, rho_ref, v_ref, acc_ref)
    new_g_ref[...] = g_ref[...] + change * (1.0 / KAPPA)
    sum_ref[...] = jnp.exp2(f_ref[...] + rho_ref[...])


def others(x, axis, size, steps):
    return [lax.ppermute(x, axis, [(i, i ^ k) for i in range(size)]) for k in steps]


def pool_src(x):
    size = lax.axis_size("src")
    if size == 4:
        return [x] + others(x, "src", size, (1, 2, 3))
    every = lax.all_gather(x, "src", axis=0)
    return [every[k] for k in range(size)]


def pool_tgt(x, join):
    size = lax.axis_size("tgt")
    if size == 8:
        x = join([x] + others(x, "tgt", size, (1,)))
        return [x] + others(x, "tgt", size, (2, 4, 6))
    every = lax.all_gather(x, "tgt", axis=0)
    return [every[k] for k in range(size)]


def body(source_points, target_points, g_init):
    dims, rows = source_points.shape
    cols = target_points.shape[1]
    n_src, n_tgt = lax.axis_size("src"), lax.axis_size("tgt")
    log_nt, log_ns = math.log2(cols * n_tgt), math.log2(rows * n_src)
    depth = 6 * dims + 16
    row, col, square = vmem((1, rows)), vmem((1, cols)), vmem((rows, LANES))

    g = g_init.reshape(1, cols)
    a, own, g = pl.pallas_call(
        functools.partial(prepare, n_src),
        out_shape=(vmem((rows, depth), bf16), vmem(target_points.shape), col),
        in_specs=[VMEM] * 3,
        out_specs=(VMEM,) * 3,
        compiler_params=PARAMS,
    )(source_points, target_points, g)
    if n_src == 4:
        blocks = [own] + others(target_points, "src", n_src, (1, 2, 3))
    else:
        blocks = [lax.all_gather(target_points, "src", axis=0, tiled=True)]
    e, b, rho, m = pl.pallas_call(
        functools.partial(build, len(blocks)),
        out_shape=(vmem((rows, cols)), vmem((depth, cols), bf16), row, row),
        in_specs=[VMEM] * (2 + len(blocks)),
        out_specs=(VMEM,) * 4,
        scratch_shapes=[square, square],
        compiler_params=PARAMS,
    )(pin(a), pin(g), *map(pin, blocks))
    a, e, b, m, g = pin(a), pin(e), pin(b), pin(m), pin(g)

    def columns(rho, outs):
        parts = pool_tgt(rho, lse2)
        return pl.pallas_call(
            functools.partial(column_pass, len(parts), log_nt),
            out_shape=outs,
            in_specs=[VMEM] * (len(parts) + 4),
            out_specs=(VMEM,) * len(outs),
            scratch_shapes=[square, col],
            compiler_params=PARAMS,
        )(*map(pin, parts), m, e, a, b)

    (lam,) = columns(rho, (col,))
    parts = pool_src(lam)
    rho = pl.pallas_call(
        functools.partial(row_pass, len(parts), log_ns),
        out_shape=row,
        in_specs=[VMEM] * (len(parts) + 4),
        out_specs=VMEM,
        scratch_shapes=[col, square],
        compiler_params=PARAMS,
    )(*map(pin, parts), m, e, a, b)
    lam, f = columns(rho, (col, row))
    parts = pool_src(lam)
    total, g_pot = pl.pallas_call(
        functools.partial(marginal_pass, len(parts), log_ns),
        out_shape=(row, col),
        in_specs=[VMEM] * (len(parts) + 6),
        out_specs=(VMEM, VMEM),
        scratch_shapes=[row, col, square],
        compiler_params=PARAMS,
    )(*map(pin, parts), m, e, a, b, pin(f), g)
    marginal = sum(pool_tgt(total, sum)) * (1.0 / (cols * n_tgt))
    f_pot = jnp.sum(source_points * source_points, axis=0) + f.reshape(rows) * (1.0 / KAPPA)
    return f_pot, g_pot.reshape(cols), marginal.reshape(rows)


def solution(mesh):
    in_specs = (P(None, "src"), P("src", "tgt"), P("tgt"))
    out_specs = (P("src"), P("tgt"), P("src"))
    return jax.shard_map(body, mesh=mesh, in_specs=in_specs, out_specs=out_specs, check_vma=False)
```

```python
import functools
import math

import jax
import jax.numpy as jnp
from jax import lax
from jax.experimental import pallas as pl
from jax.experimental.pallas import tpu as pltpu
from jax.sharding import PartitionSpec as P

epsilon = 0.05
KAPPA = math.log2(math.e) / epsilon
LANES = 128
ROW_BLOCK = 512
COL_BLOCK = 256
COL_WIDTH = 1024
ROW_HEIGHT = 128

f32 = jnp.float32
bf16 = jnp.bfloat16
VMEM = pl.BlockSpec(memory_space=pltpu.VMEM)
PARAMS = pltpu.CompilerParams(vmem_limit_bytes=16 * 2**20)


HBM = pl.BlockSpec(memory_space=pltpu.HBM)


def vmem(shape, dtype=f32):
    return pltpu.VMEM(shape, dtype)


def pin(x):
    return pltpu.with_memory_space_constraint(x, pltpu.VMEM)


def split(x):
    first = x.astype(bf16)
    rest = x - first.astype(f32)
    second = rest.astype(bf16)
    third = (rest - second.astype(f32)).astype(bf16)
    return first, second, third


def to_lanes(ref, reduce, out_ref):
    for k in range(out_ref.shape[0]):
        part = ref[k * LANES : (k + 1) * LANES, :].T
        out_ref[k : k + 1, :] = reduce(part, axis=0, keepdims=True)


def to_rows(x, out_ref):
    for k in range(x.shape[0]):
        out_ref[k * LANES : (k + 1) * LANES, :] = jnp.broadcast_to(x[k : k + 1, :], (LANES, LANES)).T


def every(*conditions):
    least = [jnp.min(jnp.where(c, 1.0, 0.0), axis=0, keepdims=True) for c in conditions]
    return jnp.min(functools.reduce(jnp.minimum, least)) > 0.5


def total_of(x):
    return jnp.sum(jnp.sum(x, axis=0, keepdims=True), axis=1, keepdims=True)


def lse2(parts):
    top = functools.reduce(jnp.maximum, parts)
    return top + jnp.log2(sum(jnp.exp2(p - top) for p in parts))


def scores(a_ref, b_ref, row, rows, col, cols):
    return jnp.dot(
        a_ref[pl.ds(row, rows), :], b_ref[:, pl.ds(col, cols)], preferred_element_type=f32
    )


def tiles(width):
    return range(0, width, LANES)


def prepare(n_src, src_ref, t_ref, g_ref, g2_ref, a_ref, own_ref, start_ref, start2_ref, square_ref):
    own_ref[...] = t_ref[...]
    start_ref[...] = g_ref[...]
    start2_ref[...] = g2_ref[...]
    dims, rows = src_ref.shape
    square = jnp.sum(src_ref[...] * src_ref[...], axis=0, keepdims=True)
    for k in range(rows // LANES):
        square_ref[k : k + 1, :] = square[:, k * LANES : (k + 1) * LANES]
    if n_src == 4:
        me, each = lax.axis_index("src"), dims // n_src
        points = jnp.concatenate(
            [src_ref[pl.ds(pl.multiple_of((me ^ k) * each, each), each), :] for k in range(n_src)],
            axis=0,
        )
    else:
        points = src_ref[...]
    s1, s2, s3 = (x.astype(f32) for x in split(points * (2.0 * KAPPA)))
    last = (lax.broadcasted_iota(jnp.int32, (16, rows), 0) < 3).astype(f32)
    a_ref[...] = jnp.concatenate([s1, s1, s2, s1, s3, s2, last], axis=0).T.astype(bf16)


def build(n_blocks, *refs):
    a_ref, g_ref = refs[:2]
    blocks = refs[2 : 2 + n_blocks]
    e_ref, b_ref, rho_ref, m_ref, acc_ref, shift_ref = refs[2 + n_blocks :]
    rows, cols = e_ref.shape
    dims = sum(ref.shape[0] for ref in blocks)
    points = jnp.concatenate([ref[...] for ref in blocks], axis=0)
    t1, t2, t3 = split(points)
    for k, part in enumerate((t1, t2, t1, t3, t1, t2)):
        b_ref[k * dims : (k + 1) * dims, :] = part
    offset = KAPPA * (g_ref[...] - jnp.sum(points * points, axis=0, keepdims=True))
    o1, o2, o3 = (x.astype(f32) for x in split(offset))
    fill = jnp.zeros((13, cols), f32)
    b_ref[6 * dims :, :] = jnp.concatenate([o1, o2, o3, fill], axis=0).astype(bf16)

    def block(i, wide):
        row = pl.multiple_of(i * ROW_BLOCK, ROW_BLOCK)
        here = pl.ds(row, ROW_BLOCK)

        def top(col):
            s = scores(a_ref, b_ref, row, ROW_BLOCK, col, COL_BLOCK)
            return s, functools.reduce(jnp.maximum, [s[:, t : t + LANES] for t in tiles(COL_BLOCK)])

        def spread(best):
            return jnp.broadcast_to(jnp.max(best, axis=1, keepdims=True), best.shape)

        if wide:
            best = lax.fori_loop(
                1,
                cols // COL_BLOCK,
                lambda c, best: jnp.maximum(best, top(pl.multiple_of(c * COL_BLOCK, COL_BLOCK))[1]),
                top(0)[1],
            )
            shift_ref[here, :] = spread(best)
        for col in range(0, cols, COL_BLOCK):
            if col == 0 and not wide:
                s, best = top(0)
                shift = spread(best)
                shift_ref[here, :] = shift
            else:
                s = scores(a_ref, b_ref, row, ROW_BLOCK, col, COL_BLOCK)
                shift = shift_ref[here, :]
            acc = acc_ref[here, :] if col else 0.0
            for t in tiles(COL_BLOCK):
                e = jnp.exp2(s[:, t : t + LANES] - shift)
                e_ref[here, col + t : col + t + LANES] = e
                acc = acc + e
            acc_ref[here, :] = acc

    def run(wide):
        lax.fori_loop(0, rows // ROW_BLOCK, lambda i, _: block(i, wide), None)
        to_lanes(acc_ref, jnp.sum, rho_ref)
        to_lanes(shift_ref, jnp.max, m_ref)
        total = rho_ref[...]
        rho_ref[...] = m_ref[...] + jnp.log2(total)
        return total

    total = run(False)
    fine = jnp.max(total) < 2.0**100

    @pl.when(jnp.logical_not(fine))
    def _():
        run(True)


def column_sums(e_ref, u_ref, q_ref):
    rows, cols = e_ref.shape
    for col in range(0, cols, COL_WIDTH):
        acc = [0.0] * (COL_WIDTH // LANES)
        for row in range(0, rows, 8):
            u = u_ref[row : row + 8, :]
            for k, t in enumerate(tiles(COL_WIDTH)):
                acc[k] = acc[k] + e_ref[row : row + 8, col + t : col + t + LANES] * u
        for k, t in enumerate(tiles(COL_WIDTH)):
            at = (col + t) // LANES
            q_ref[at : at + 1, :] = jnp.sum(acc[k], axis=0, keepdims=True)


def row_sums(e_ref, v_ref, acc_ref):
    rows, cols = e_ref.shape
    for row in range(0, rows, ROW_HEIGHT):
        acc = [0.0] * (ROW_HEIGHT // 8)
        for t in tiles(cols):
            v = jnp.broadcast_to(v_ref[t // LANES : t // LANES + 1, :], (8, LANES))
            for k in range(ROW_HEIGHT // 8):
                acc[k] = acc[k] + e_ref[row + 8 * k : row + 8 * k + 8, t : t + LANES] * v
        for k in range(ROW_HEIGHT // 8):
            acc_ref[row + 8 * k : row + 8 * k + 8, :] = acc[k]


def column_pass(n_parts, log_nt, *refs):
    parts = refs[:n_parts]
    m_ref, e_ref, a_ref, b_ref, *rest, u_ref = refs[n_parts:]
    rows, cols = e_ref.shape
    pot = log_nt - lse2([ref[...] for ref in parts])
    copy = None
    if len(rest) == 1:
        (lam_ref,) = rest
    else:
        square_ref, lam_ref, f_ref, out_ref, stage_ref, sem = rest
        f_ref[...] = pot
        stage_ref[...] = square_ref[...] + pot * (1.0 / KAPPA)
        copy = pltpu.make_async_copy(stage_ref, out_ref, sem)
        copy.start()
    power = pot + m_ref[...]
    u = jnp.exp2(power)
    to_rows(u, u_ref)
    column_sums(e_ref, u_ref, lam_ref)
    q = lam_ref[...]
    lam_ref[...] = jnp.log2(q)
    least = jnp.maximum(total_of(u) * 2.0**-106, 2.0**-96)
    fine = every(power > -100.0, (q >= least) & (q < 2.0**120))

    @pl.when(jnp.logical_not(fine))
    def _():
        to_rows(pot, u_ref)

        def block(c, _):
            col = pl.multiple_of(c * LANES, LANES)

            def shifted(i):
                row = pl.multiple_of(i * LANES, LANES)
                return scores(a_ref, b_ref, row, LANES, col, LANES) + u_ref[pl.ds(row, LANES), :]

            top = lax.fori_loop(
                0,
                rows // LANES,
                lambda i, best: jnp.maximum(best, jnp.max(shifted(i), axis=0, keepdims=True)),
                jnp.full((1, LANES), -jnp.inf, f32),
            )
            total = lax.fori_loop(
                0,
                rows // LANES,
                lambda i, acc: acc + jnp.sum(jnp.exp2(shifted(i) - top), axis=0, keepdims=True),
                jnp.zeros((1, LANES), f32),
            )
            lam_ref[pl.ds(c, 1), :] = top + jnp.log2(total)
            return 0

        lax.fori_loop(0, cols // LANES, block, 0)

    if copy is not None:
        copy.wait()


def row_log_sums(change, m_ref, e_ref, a_ref, b_ref, rho_ref, v_ref, acc_ref):
    rows, cols = e_ref.shape
    v = jnp.exp2(change)
    v_ref[...] = v
    row_sums(e_ref, v_ref, acc_ref)
    to_lanes(acc_ref, jnp.sum, rho_ref)
    r = rho_ref[...]
    rho_ref[...] = m_ref[...] + jnp.log2(r)
    least = jnp.maximum(total_of(v) * 2.0**-106, 2.0**-94)
    fine = every(change > -100.0, (r >= least) & (r < 2.0**120))

    @pl.when(jnp.logical_not(fine))
    def _():
        v_ref[...] = change

        def block(i, _):
            row = pl.multiple_of(i * LANES, LANES)

            def shifted(c):
                col = pl.multiple_of(c * LANES, LANES)
                return scores(a_ref, b_ref, row, LANES, col, LANES) + v_ref[pl.ds(c, 1), :]

            top = lax.fori_loop(
                0,
                cols // LANES,
                lambda c, best: jnp.maximum(best, jnp.max(shifted(c), axis=1, keepdims=True)),
                jnp.full((LANES, 1), -jnp.inf, f32),
            )
            total = lax.fori_loop(
                0,
                cols // LANES,
                lambda c, acc: acc + jnp.sum(jnp.exp2(shifted(c) - top), axis=1, keepdims=True),
                jnp.zeros((LANES, 1), f32),
            )
            value = jnp.broadcast_to(top + jnp.log2(total), (LANES, LANES))
            rho_ref[pl.ds(i, 1), :] = jnp.max(value.T, axis=0, keepdims=True)
            return 0

        lax.fori_loop(0, rows // LANES, block, 0)


def row_pass(n_parts, log_ns, *refs):
    parts = refs[:n_parts]
    change = log_ns - lse2([ref[...] for ref in parts])
    row_log_sums(change, *refs[n_parts:])


def marginal_pass(n_parts, log_ns, *refs):
    parts = refs[:n_parts]
    m_ref, e_ref, a_ref, b_ref, f_ref, g_ref, sum_ref, out_ref, rho_ref, v_ref, acc_ref, stage_ref, sem = refs[n_parts:]
    change = log_ns - lse2([ref[...] for ref in parts])
    stage_ref[...] = g_ref[...] + change * (1.0 / KAPPA)
    copy = pltpu.make_async_copy(stage_ref, out_ref, sem)
    copy.start()
    row_log_sums(change, m_ref, e_ref, a_ref, b_ref, rho_ref, v_ref, acc_ref)
    sum_ref[...] = jnp.exp2(f_ref[...] + rho_ref[...])
    copy.wait()


def others(x, axis, size, steps):
    return [lax.ppermute(x, axis, [(i, i ^ k) for i in range(size)]) for k in steps]


def pool_src(x):
    size = lax.axis_size("src")
    if size == 4:
        return [x] + others(x, "src", size, (1, 2, 3))
    every = lax.all_gather(x, "src", axis=0)
    return [every[k] for k in range(size)]


def pool_tgt(x, join):
    size = lax.axis_size("tgt")
    if size == 8:
        x = join([x] + others(x, "tgt", size, (1,)))
        return [x] + others(x, "tgt", size, (3, 5, 7))
    every = lax.all_gather(x, "tgt", axis=0)
    return [every[k] for k in range(size)]


def body(source_points, target_points, g_init):
    dims, rows = source_points.shape
    cols = target_points.shape[1]
    n_src, n_tgt = lax.axis_size("src"), lax.axis_size("tgt")
    log_nt, log_ns = math.log2(cols * n_tgt), math.log2(rows * n_src)
    depth = 6 * dims + 16
    row_shape, col_shape = (rows // LANES, LANES), (cols // LANES, LANES)
    row, col, square = vmem(row_shape), vmem(col_shape), vmem((rows, LANES))

    def call(kernel, outs, scratch, *args):
        specs = [HBM if out.memory_space == pltpu.HBM else VMEM for out in outs]
        return pl.pallas_call(
            kernel,
            out_shape=tuple(outs),
            in_specs=[VMEM] * len(args),
            out_specs=tuple(specs),
            scratch_shapes=scratch,
            compiler_params=PARAMS,
        )(*args)

    a, own, g, g2, squares = call(
        functools.partial(prepare, n_src),
        (vmem((rows, depth), bf16), vmem(target_points.shape), vmem((1, cols)), col, row),
        [],
        source_points,
        target_points,
        g_init.reshape(1, cols),
        g_init.reshape(col_shape),
    )
    if n_src == 4:
        blocks = [own] + others(target_points, "src", n_src, (1, 2, 3))
    else:
        blocks = [lax.all_gather(target_points, "src", axis=0, tiled=True)]
    a = pin(a)
    e, b, rho, m = call(
        functools.partial(build, len(blocks)),
        (vmem((rows, cols)), vmem((depth, cols), bf16), row, row),
        [square, square],
        a,
        pin(g),
        *map(pin, blocks),
    )
    kept = [pin(x) for x in (m, e, a, b)]

    parts = [pin(x) for x in pool_tgt(rho, lse2)]
    (lam,) = call(functools.partial(column_pass, len(parts), log_nt), (col,), [square], *parts, *kept)
    parts = [pin(x) for x in pool_src(lam)]
    (rho,) = call(functools.partial(row_pass, len(parts), log_ns), (row,), [col, square], *parts, *kept)
    parts = [pin(x) for x in pool_tgt(rho, lse2)]
    lam, f, f_pot = call(
        functools.partial(column_pass, len(parts), log_nt),
        (col, row, pltpu.HBM(row_shape, f32)),
        [row, pltpu.SemaphoreType.DMA, square],
        *parts,
        *kept,
        pin(squares),
    )
    parts = [pin(x) for x in pool_src(lam)]
    total, g_pot = call(
        functools.partial(marginal_pass, len(parts), log_ns),
        (row, pltpu.HBM(col_shape, f32)),
        [row, col, square, col, pltpu.SemaphoreType.DMA],
        *parts,
        *kept,
        pin(f),
        pin(g2),
    )
    marginal = sum(pool_tgt(total, sum)) * (1.0 / (cols * n_tgt))
    return f_pot.reshape(rows), g_pot.reshape(cols), marginal.reshape(rows)


def solution(mesh):
    in_specs = (P(None, "src"), P("src", "tgt"), P("tgt"))
    out_specs = (P("src"), P("tgt"), P("src"))
    return jax.shard_map(body, mesh=mesh, in_specs=in_specs, out_specs=out_specs, check_vma=False)
```

```python
import functools
import math

import jax
import jax.numpy as jnp
from jax import lax
from jax.experimental import pallas as pl
from jax.experimental.pallas import tpu as pltpu
from jax.sharding import PartitionSpec as P

epsilon = 0.05
KAPPA = math.log2(math.e) / epsilon
LANES = 128
ROW_BLOCK = 512
COL_BLOCK = 256
COL_WIDTH = 1024
ROW_HEIGHT = 128

f32 = jnp.float32
bf16 = jnp.bfloat16
VMEM = pl.BlockSpec(memory_space=pltpu.VMEM)
PARAMS = pltpu.CompilerParams(vmem_limit_bytes=16 * 2**20)


HBM = pl.BlockSpec(memory_space=pltpu.HBM)


def vmem(shape, dtype=f32):
    return pltpu.VMEM(shape, dtype)


def pin(x, space=pltpu.VMEM):
    return pltpu.with_memory_space_constraint(x, space)


def split(x):
    first = x.astype(bf16)
    rest = x - first.astype(f32)
    second = rest.astype(bf16)
    third = (rest - second.astype(f32)).astype(bf16)
    return first, second, third


def to_lanes(ref, reduce, out_ref):
    for k in range(out_ref.shape[0]):
        part = ref[k * LANES : (k + 1) * LANES, :].T
        out_ref[k : k + 1, :] = reduce(part, axis=0, keepdims=True)


def to_rows(x, out_ref):
    for k in range(x.shape[0]):
        out_ref[k * LANES : (k + 1) * LANES, :] = jnp.broadcast_to(x[k : k + 1, :], (LANES, LANES)).T


def every(*conditions):
    least = [jnp.min(jnp.where(c, 1.0, 0.0), axis=0, keepdims=True) for c in conditions]
    return jnp.min(functools.reduce(jnp.minimum, least)) > 0.5


def total_of(x):
    return jnp.sum(jnp.sum(x, axis=0, keepdims=True), axis=1, keepdims=True)


def lse2(parts):
    top = functools.reduce(jnp.maximum, parts)
    return top + jnp.log2(sum(jnp.exp2(p - top) for p in parts))


def scores(a_ref, b_ref, row, rows, col, cols):
    return jnp.dot(
        a_ref[pl.ds(row, rows), :], b_ref[:, pl.ds(col, cols)], preferred_element_type=f32
    )


def tiles(width):
    return range(0, width, LANES)


def prepare(n_src, src_ref, t_ref, g_ref, g2_ref, a_ref, square_ref, start_ref, start2_ref, *rest):
    *targets, points_ref, sems = rest
    pairs = [(src_ref, points_ref), (g_ref, start_ref), (g2_ref, start2_ref)]
    if targets:
        own_ref, *halves = targets
        pairs.append((t_ref, own_ref))
        width = halves[0].shape[1]
        pairs += [(t_ref.at[:, pl.ds(k * width, width)], half) for k, half in enumerate(halves)]
    copies = [pltpu.make_async_copy(x, y, sems.at[k]) for k, (x, y) in enumerate(pairs)]
    for copy in copies:
        copy.start()
    for copy in copies:
        copy.wait()
    dims, rows = points_ref.shape
    points = points_ref[...]
    square = jnp.sum(points * points, axis=0, keepdims=True)
    for k in range(rows // LANES):
        square_ref[k : k + 1, :] = square[:, k * LANES : (k + 1) * LANES]
    if n_src == 4:
        me, each = lax.axis_index("src"), dims // n_src
        points = jnp.concatenate(
            [points_ref[pl.ds(pl.multiple_of((me ^ k) * each, each), each), :] for k in range(n_src)],
            axis=0,
        )
    s1, s2, s3 = (x.astype(f32) for x in split(points * (2.0 * KAPPA)))
    last = (lax.broadcasted_iota(jnp.int32, (16, rows), 0) < 3).astype(f32)
    a_ref[...] = jnp.concatenate([s1, s1, s2, s1, s3, s2, last], axis=0).T.astype(bf16)


def fill_right(half, g_ref, blocks, b_ref):
    cols = b_ref.shape[1]
    here = slice(half * cols, (half + 1) * cols)
    points = jnp.concatenate([ref[...] if ref.shape[1] == cols else ref[:, here] for ref in blocks], axis=0)
    dims = points.shape[0]
    t1, t2, t3 = split(points)
    for k, part in enumerate((t1, t2, t1, t3, t1, t2)):
        b_ref[k * dims : (k + 1) * dims, :] = part
    offset = KAPPA * (g_ref[:, here] - jnp.sum(points * points, axis=0, keepdims=True))
    o1, o2, o3 = (x.astype(f32) for x in split(offset))
    fill = jnp.zeros((13, cols), f32)
    b_ref[6 * dims :, :] = jnp.concatenate([o1, o2, o3, fill], axis=0).astype(bf16)


def row_top(a_ref, b_ref, row, col):
    s = scores(a_ref, b_ref, row, ROW_BLOCK, col, COL_BLOCK)
    return s, functools.reduce(jnp.maximum, [s[:, t : t + LANES] for t in tiles(COL_BLOCK)])


def spread(best):
    return jnp.broadcast_to(jnp.max(best, axis=1, keepdims=True), best.shape)


def fill_half(first, a_ref, b_ref, e_ref, shift_ref, start_ref, acc_ref):
    rows, cols = e_ref.shape

    def block(i, _):
        row = pl.multiple_of(i * ROW_BLOCK, ROW_BLOCK)
        here = pl.ds(row, ROW_BLOCK)
        for col in range(0, cols, COL_BLOCK):
            if first and col == 0:
                s, best = row_top(a_ref, b_ref, row, col)
                shift = spread(best)
                shift_ref[here, :] = shift
            else:
                s = scores(a_ref, b_ref, row, ROW_BLOCK, col, COL_BLOCK)
                shift = shift_ref[here, :]
            if col:
                acc = acc_ref[here, :]
            else:
                acc = start_ref[here, :] if start_ref is not None else 0.0
            for t in tiles(COL_BLOCK):
                e = jnp.exp2(s[:, t : t + LANES] - shift)
                e_ref[here, col + t : col + t + LANES] = e
                acc = acc + e
            acc_ref[here, :] = acc

    lax.fori_loop(0, rows // ROW_BLOCK, block, None)


def build_first(n_blocks, *refs):
    a_ref, g_ref = refs[:2]
    blocks = refs[2 : 2 + n_blocks]
    e_ref, b_ref, shift_ref, acc_ref = refs[2 + n_blocks :]
    fill_right(0, g_ref, blocks, b_ref)
    fill_half(True, a_ref, b_ref, e_ref, shift_ref, None, acc_ref)


def build_second(n_blocks, *refs):
    a_ref, g_ref = refs[:2]
    blocks = refs[2 : 2 + n_blocks]
    _, b0_ref, shift_ref, start_ref = refs[2 + n_blocks : 6 + n_blocks]
    e0_ref, e_ref, b_ref, rho_ref, m_ref, acc_ref, exact_ref = refs[6 + n_blocks :]
    fill_right(1, g_ref, blocks, b_ref)
    fill_half(False, a_ref, b_ref, e_ref, shift_ref, start_ref, acc_ref)

    def finish(shift_ref):
        to_lanes(acc_ref, jnp.sum, rho_ref)
        to_lanes(shift_ref, jnp.max, m_ref)
        total = rho_ref[...]
        rho_ref[...] = m_ref[...] + jnp.log2(total)
        return total

    fine = every(finish(shift_ref) < 2.0**100)

    @pl.when(jnp.logical_not(fine))
    def _():
        def block(i, _):
            row = pl.multiple_of(i * ROW_BLOCK, ROW_BLOCK)
            best = jnp.full((ROW_BLOCK, LANES), -jnp.inf, f32)
            for part in (b0_ref, b_ref):
                best = lax.fori_loop(
                    0,
                    part.shape[1] // COL_BLOCK,
                    lambda c, best: jnp.maximum(
                        best, row_top(a_ref, part, row, pl.multiple_of(c * COL_BLOCK, COL_BLOCK))[1]
                    ),
                    best,
                )
            exact_ref[pl.ds(row, ROW_BLOCK), :] = spread(best)

        lax.fori_loop(0, e_ref.shape[0] // ROW_BLOCK, block, None)
        fill_half(False, a_ref, b0_ref, e0_ref, exact_ref, None, acc_ref)
        fill_half(False, a_ref, b_ref, e_ref, exact_ref, acc_ref, acc_ref)
        finish(exact_ref)


def column_sums(e_refs, u_ref, q_ref):
    at = 0
    for e_ref in e_refs:
        rows, cols = e_ref.shape
        for col in range(0, cols, COL_WIDTH):
            acc = [0.0] * (COL_WIDTH // LANES)
            for row in range(0, rows, 8):
                u = u_ref[row : row + 8, :]
                for k, t in enumerate(tiles(COL_WIDTH)):
                    acc[k] = acc[k] + e_ref[row : row + 8, col + t : col + t + LANES] * u
            for part in acc:
                q_ref[at : at + 1, :] = jnp.sum(part, axis=0, keepdims=True)
                at += 1


def row_sums(e_refs, v_ref, acc_ref):
    for row in range(0, acc_ref.shape[0], ROW_HEIGHT):
        acc = [0.0] * (ROW_HEIGHT // 8)
        at = 0
        for e_ref in e_refs:
            for t in tiles(e_ref.shape[1]):
                v = jnp.broadcast_to(v_ref[at : at + 1, :], (8, LANES))
                at += 1
                for k in range(ROW_HEIGHT // 8):
                    acc[k] = acc[k] + e_ref[row + 8 * k : row + 8 * k + 8, t : t + LANES] * v
        for k in range(ROW_HEIGHT // 8):
            acc_ref[row + 8 * k : row + 8 * k + 8, :] = acc[k]


def column_pass(n_parts, log_nt, *refs):
    parts = refs[:n_parts]
    m_ref, a_ref, e0_ref, e1_ref, b0_ref, b1_ref, lam_ref, *f_ref, u_ref = refs[n_parts:]
    rows = a_ref.shape[0]
    pot = log_nt - lse2([ref[...] for ref in parts])
    for ref in f_ref:
        ref[...] = pot
    power = pot + m_ref[...]
    u = jnp.exp2(power)
    to_rows(u, u_ref)
    column_sums((e0_ref, e1_ref), u_ref, lam_ref)
    q = lam_ref[...]
    lam_ref[...] = jnp.log2(q)
    least = jnp.maximum(total_of(u) * 2.0**-106, 2.0**-96)
    fine = every(power > -100.0, (q >= least) & (q < 2.0**120))

    @pl.when(jnp.logical_not(fine))
    def _():
        to_rows(pot, u_ref)
        first = 0
        for b_ref in (b0_ref, b1_ref):

            def block(c, _):
                col = pl.multiple_of(c * LANES, LANES)

                def shifted(i):
                    row = pl.multiple_of(i * LANES, LANES)
                    return scores(a_ref, b_ref, row, LANES, col, LANES) + u_ref[pl.ds(row, LANES), :]

                top = lax.fori_loop(
                    0,
                    rows // LANES,
                    lambda i, best: jnp.maximum(best, jnp.max(shifted(i), axis=0, keepdims=True)),
                    jnp.full((1, LANES), -jnp.inf, f32),
                )
                total = lax.fori_loop(
                    0,
                    rows // LANES,
                    lambda i, acc: acc + jnp.sum(jnp.exp2(shifted(i) - top), axis=0, keepdims=True),
                    jnp.zeros((1, LANES), f32),
                )
                lam_ref[pl.ds(first + c, 1), :] = top + jnp.log2(total)

            lax.fori_loop(0, b_ref.shape[1] // LANES, block, None)
            first += b_ref.shape[1] // LANES


def row_log_sums(change, m_ref, a_ref, e0_ref, e1_ref, b0_ref, b1_ref, rho_ref, v_ref, acc_ref):
    v = jnp.exp2(change)
    v_ref[...] = v
    row_sums((e0_ref, e1_ref), v_ref, acc_ref)
    to_lanes(acc_ref, jnp.sum, rho_ref)
    r = rho_ref[...]
    rho_ref[...] = m_ref[...] + jnp.log2(r)
    least = jnp.maximum(total_of(v) * 2.0**-106, 2.0**-94)
    fine = every(change > -100.0, (r >= least) & (r < 2.0**120))

    @pl.when(jnp.logical_not(fine))
    def _():
        v_ref[...] = change

        def block(i, _):
            row = pl.multiple_of(i * LANES, LANES)

            def over_columns(step, value):
                first = 0
                for b_ref in (b0_ref, b1_ref):

                    def body(c, value):
                        col = pl.multiple_of(c * LANES, LANES)
                        s = scores(a_ref, b_ref, row, LANES, col, LANES) + v_ref[pl.ds(first + c, 1), :]
                        return step(value, s)

                    value = lax.fori_loop(0, b_ref.shape[1] // LANES, body, value)
                    first += b_ref.shape[1] // LANES
                return value

            top = over_columns(
                lambda best, s: jnp.maximum(best, jnp.max(s, axis=1, keepdims=True)),
                jnp.full((LANES, 1), -jnp.inf, f32),
            )
            total = over_columns(
                lambda acc, s: acc + jnp.sum(jnp.exp2(s - top), axis=1, keepdims=True),
                jnp.zeros((LANES, 1), f32),
            )
            value = jnp.broadcast_to(top + jnp.log2(total), (LANES, LANES))
            rho_ref[pl.ds(i, 1), :] = jnp.max(value.T, axis=0, keepdims=True)

        lax.fori_loop(0, a_ref.shape[0] // LANES, block, None)


def row_pass(n_parts, log_ns, *refs):
    parts = refs[:n_parts]
    change = log_ns - lse2([ref[...] for ref in parts])
    row_log_sums(change, *refs[n_parts:])


def marginal_pass(n_parts, log_ns, *refs):
    parts = refs[:n_parts]
    *kept, f_ref, g_ref, _, sum_ref, new_ref, rho_ref, v_ref, acc_ref = refs[n_parts:]
    change = log_ns - lse2([ref[...] for ref in parts])
    new_ref[...] = g_ref[...] + change * (1.0 / KAPPA)
    row_log_sums(change, *kept, rho_ref, v_ref, acc_ref)
    sum_ref[...] = jnp.exp2(f_ref[...] + rho_ref[...])


def others(x, axis, size, steps):
    return [lax.ppermute(x, axis, [(i, i ^ k) for i in range(size)]) for k in steps]


def pool_src(x):
    size = lax.axis_size("src")
    if size == 4:
        return [x] + others(x, "src", size, (1, 2, 3))
    every = lax.all_gather(x, "src", axis=0)
    return [every[k] for k in range(size)]


def pool_tgt(x, join):
    size = lax.axis_size("tgt")
    if size == 8:
        x = join([x] + others(x, "tgt", size, (1,)))
        return [x] + others(x, "tgt", size, (3, 5, 7))
    every = lax.all_gather(x, "tgt", axis=0)
    return [every[k] for k in range(size)]


def body(source_points, target_points, g_init):
    dims, rows = source_points.shape
    cols = target_points.shape[1]
    half = cols // 2
    n_src, n_tgt = lax.axis_size("src"), lax.axis_size("tgt")
    log_nt, log_ns = math.log2(cols * n_tgt), math.log2(rows * n_src)
    depth = 6 * dims + 16
    row_shape, col_shape = (rows // LANES, LANES), (cols // LANES, LANES)
    row, col, square = vmem(row_shape), vmem(col_shape), vmem((rows, LANES))
    e_half, b_half = vmem((rows, half)), vmem((depth, half), bf16)

    def call(kernel, outs, scratch, *args, in_hbm=(), aliases={}):
        return pl.pallas_call(
            kernel,
            out_shape=tuple(outs),
            in_specs=[HBM if k in in_hbm else VMEM for k in range(len(args))],
            out_specs=(VMEM,) * len(outs),
            scratch_shapes=scratch,
            input_output_aliases=aliases,
            compiler_params=PARAMS,
        )(*args)

    split_gather = n_src == 4
    targets = (vmem(target_points.shape),) + (vmem((target_points.shape[0], half)),) * 2
    a, squares, g, g2, *own = call(
        functools.partial(prepare, n_src),
        (vmem((rows, depth), bf16), row, vmem((1, cols)), col) + (targets if split_gather else ()),
        [vmem(source_points.shape), pltpu.SemaphoreType.DMA((6,))],
        *(
            pin(x, pltpu.HBM)
            for x in (source_points, target_points, g_init.reshape(1, cols), g_init.reshape(col_shape))
        ),
        in_hbm=(0, 1, 2, 3),
    )
    if split_gather:
        far, near = others(target_points, "src", n_src, (3, 2))
        first, second = (others(pin(x), "src", n_src, (1,))[0] for x in own[1:])
        blocks = [[own[0], x, near, far] for x in (first, second)]
    else:
        blocks = [[lax.all_gather(target_points, "src", axis=0, tiled=True)]] * 2
    blocks = [[pin(x) for x in part] for part in blocks]
    a, g = pin(a), pin(g)
    e0, b0, shift, acc = call(
        functools.partial(build_first, len(blocks[0])),
        (e_half, b_half, square, square),
        [],
        a,
        g,
        *blocks[0],
    )
    b0 = pin(b0)
    e0, e1, b1, rho, m = call(
        functools.partial(build_second, len(blocks[1])),
        (e_half, e_half, b_half, row, row),
        [square, square],
        a,
        g,
        *blocks[1],
        pin(e0),
        b0,
        pin(shift),
        pin(acc),
        aliases={2 + len(blocks[1]): 0},
    )
    kept = [pin(m), a, pin(e0), pin(e1), b0, pin(b1)]

    parts = [pin(x) for x in pool_tgt(rho, lse2)]
    (lam,) = call(functools.partial(column_pass, len(parts), log_nt), (col,), [square], *parts, *kept)
    parts = [pin(x) for x in pool_src(lam)]
    (rho,) = call(functools.partial(row_pass, len(parts), log_ns), (row,), [col, square], *parts, *kept)
    parts = [pin(x) for x in pool_tgt(rho, lse2)]
    lam, f = call(functools.partial(column_pass, len(parts), log_nt), (col, row), [square], *parts, *kept)
    parts = [pin(x) for x in pool_src(lam)]
    f_pot = squares + f * (1.0 / KAPPA)
    args = parts + kept + [pin(f), pin(g2), f_pot]
    total, g_pot = call(
        functools.partial(marginal_pass, len(parts), log_ns),
        (row, col),
        [row, col, square],
        *args,
        in_hbm=(len(args) - 1,),
    )
    marginal = sum(pool_tgt(total, sum)) * (1.0 / (cols * n_tgt))
    return f_pot.reshape(rows), g_pot.reshape(cols), marginal.reshape(rows)


def solution(mesh):
    in_specs = (P(None, "src"), P("src", "tgt"), P("tgt"))
    out_specs = (P("src"), P("tgt"), P("src"))
    return jax.shard_map(body, mesh=mesh, in_specs=in_specs, out_specs=out_specs, check_vma=False)
```

```python
import functools
import math

import jax
import jax.numpy as jnp
from jax import lax
from jax.experimental import pallas as pl
from jax.experimental.pallas import tpu as pltpu
from jax.sharding import PartitionSpec as P

epsilon = 0.05
KAPPA = math.log2(math.e) / epsilon
LANES = 128
ROW_BLOCK = 512
COL_BLOCK = 256
COL_WIDTH = 1024
ROW_HEIGHT = 128

f32 = jnp.float32
bf16 = jnp.bfloat16
VMEM = pl.BlockSpec(memory_space=pltpu.VMEM)
PARAMS = pltpu.CompilerParams(vmem_limit_bytes=16 * 2**20)


HBM = pl.BlockSpec(memory_space=pltpu.HBM)


def vmem(shape, dtype=f32):
    return pltpu.VMEM(shape, dtype)


def pin(x, space=pltpu.VMEM):
    return pltpu.with_memory_space_constraint(x, space)


def split(x):
    first = x.astype(bf16)
    rest = x - first.astype(f32)
    second = rest.astype(bf16)
    third = (rest - second.astype(f32)).astype(bf16)
    return first, second, third


def to_lanes(ref, reduce, out_ref):
    for k in range(out_ref.shape[0]):
        part = ref[k * LANES : (k + 1) * LANES, :].T
        out_ref[k : k + 1, :] = reduce(part, axis=0, keepdims=True)


def to_rows(x, out_ref):
    for k in range(x.shape[0]):
        out_ref[k * LANES : (k + 1) * LANES, :] = jnp.broadcast_to(x[k : k + 1, :], (LANES, LANES)).T


def every(*conditions):
    least = [jnp.min(jnp.where(c, 1.0, 0.0), axis=0, keepdims=True) for c in conditions]
    return jnp.min(functools.reduce(jnp.minimum, least)) > 0.5


def total_of(x):
    return jnp.sum(jnp.sum(x, axis=0, keepdims=True), axis=1, keepdims=True)


def lse2(parts):
    top = functools.reduce(jnp.maximum, parts)
    return top + jnp.log2(sum(jnp.exp2(p - top) for p in parts))


def scores(a_ref, b_ref, row, rows, col, cols):
    return jnp.dot(
        a_ref[pl.ds(row, rows), :], b_ref[:, pl.ds(col, cols)], preferred_element_type=f32
    )


def tiles(width):
    return range(0, width, LANES)


def prepare(n_src, src_ref, t_ref, g_ref, g2_ref, a_ref, square_ref, start_ref, start2_ref, *rest):
    *targets, points_ref, sems = rest
    pairs = [(src_ref, points_ref), (g_ref, start_ref), (g2_ref, start2_ref)]
    if targets:
        own_ref, *halves = targets
        pairs.append((t_ref, own_ref))
        width = halves[0].shape[1]
        pairs += [(t_ref.at[:, pl.ds(k * width, width)], half) for k, half in enumerate(halves)]
    copies = [pltpu.make_async_copy(x, y, sems.at[k]) for k, (x, y) in enumerate(pairs)]
    for copy in copies:
        copy.start()
    for copy in copies:
        copy.wait()
    dims, rows = points_ref.shape
    points = points_ref[...]
    square = jnp.sum(points * points, axis=0, keepdims=True)
    for k in range(rows // LANES):
        square_ref[k : k + 1, :] = square[:, k * LANES : (k + 1) * LANES]
    if n_src == 4:
        me, each = lax.axis_index("src"), dims // n_src
        points = jnp.concatenate(
            [points_ref[pl.ds(pl.multiple_of((me ^ k) * each, each), each), :] for k in range(n_src)],
            axis=0,
        )
    s1, s2, s3 = (x.astype(f32) for x in split(points * (2.0 * KAPPA)))
    last = (lax.broadcasted_iota(jnp.int32, (16, rows), 0) < 3).astype(f32)
    a_ref[...] = jnp.concatenate([s1, s1, s2, s1, s3, s2, last], axis=0).T.astype(bf16)


def fill_right(half, g_ref, blocks, b_ref):
    cols = b_ref.shape[1]
    here = slice(half * cols, (half + 1) * cols)
    points = jnp.concatenate([ref[...] if ref.shape[1] == cols else ref[:, here] for ref in blocks], axis=0)
    dims = points.shape[0]
    t1, t2, t3 = split(points)
    for k, part in enumerate((t1, t2, t1, t3, t1, t2)):
        b_ref[k * dims : (k + 1) * dims, :] = part
    offset = KAPPA * (g_ref[:, here] - jnp.sum(points * points, axis=0, keepdims=True))
    o1, o2, o3 = (x.astype(f32) for x in split(offset))
    fill = jnp.zeros((13, cols), f32)
    b_ref[6 * dims :, :] = jnp.concatenate([o1, o2, o3, fill], axis=0).astype(bf16)


def row_top(a_ref, b_ref, row, col):
    s = scores(a_ref, b_ref, row, ROW_BLOCK, col, COL_BLOCK)
    return s, functools.reduce(jnp.maximum, [s[:, t : t + LANES] for t in tiles(COL_BLOCK)])


def spread(best):
    return jnp.broadcast_to(jnp.max(best, axis=1, keepdims=True), best.shape)


def fill_half(first, a_ref, b_ref, e_ref, shift_ref, start_ref, acc_ref):
    rows, cols = e_ref.shape

    def block(i, _):
        row = pl.multiple_of(i * ROW_BLOCK, ROW_BLOCK)
        here = pl.ds(row, ROW_BLOCK)
        for col in range(0, cols, COL_BLOCK):
            if first and col == 0:
                s, best = row_top(a_ref, b_ref, row, col)
                shift = spread(best)
                shift_ref[here, :] = shift
            else:
                s = scores(a_ref, b_ref, row, ROW_BLOCK, col, COL_BLOCK)
                shift = shift_ref[here, :]
            if col:
                acc = acc_ref[here, :]
            else:
                acc = start_ref[here, :] if start_ref is not None else 0.0
            for t in tiles(COL_BLOCK):
                e = jnp.exp2(s[:, t : t + LANES] - shift)
                e_ref[here, col + t : col + t + LANES] = e
                acc = acc + e
            acc_ref[here, :] = acc

    lax.fori_loop(0, rows // ROW_BLOCK, block, None)


def build_first(n_blocks, *refs):
    a_ref, g_ref = refs[:2]
    blocks = refs[2 : 2 + n_blocks]
    e_ref, b_ref, shift_ref, acc_ref = refs[2 + n_blocks :]
    fill_right(0, g_ref, blocks, b_ref)
    fill_half(True, a_ref, b_ref, e_ref, shift_ref, None, acc_ref)


def build_second(n_blocks, *refs):
    a_ref, g_ref = refs[:2]
    blocks = refs[2 : 2 + n_blocks]
    _, b0_ref, shift_ref, start_ref = refs[2 + n_blocks : 6 + n_blocks]
    e0_ref, e_ref, b_ref, rho_ref, m_ref, acc_ref, exact_ref = refs[6 + n_blocks :]
    fill_right(1, g_ref, blocks, b_ref)
    fill_half(False, a_ref, b_ref, e_ref, shift_ref, start_ref, acc_ref)

    def finish(shift_ref):
        to_lanes(acc_ref, jnp.sum, rho_ref)
        to_lanes(shift_ref, jnp.max, m_ref)
        total = rho_ref[...]
        rho_ref[...] = m_ref[...] + jnp.log2(total)
        return total

    fine = every(finish(shift_ref) < 2.0**100)

    @pl.when(jnp.logical_not(fine))
    def _():
        def block(i, _):
            row = pl.multiple_of(i * ROW_BLOCK, ROW_BLOCK)
            best = jnp.full((ROW_BLOCK, LANES), -jnp.inf, f32)
            for part in (b0_ref, b_ref):
                best = lax.fori_loop(
                    0,
                    part.shape[1] // COL_BLOCK,
                    lambda c, best: jnp.maximum(
                        best, row_top(a_ref, part, row, pl.multiple_of(c * COL_BLOCK, COL_BLOCK))[1]
                    ),
                    best,
                )
            exact_ref[pl.ds(row, ROW_BLOCK), :] = spread(best)

        lax.fori_loop(0, e_ref.shape[0] // ROW_BLOCK, block, None)
        fill_half(False, a_ref, b0_ref, e0_ref, exact_ref, None, acc_ref)
        fill_half(False, a_ref, b_ref, e_ref, exact_ref, acc_ref, acc_ref)
        finish(exact_ref)


def column_sums(e_refs, u_ref, q_ref):
    at = 0
    for e_ref in e_refs:
        rows, cols = e_ref.shape
        for col in range(0, cols, COL_WIDTH):
            acc = [0.0] * (COL_WIDTH // LANES)
            for row in range(0, rows, 8):
                u = u_ref[row : row + 8, :]
                for k, t in enumerate(tiles(COL_WIDTH)):
                    acc[k] = acc[k] + e_ref[row : row + 8, col + t : col + t + LANES] * u
            for part in acc:
                q_ref[at : at + 1, :] = jnp.sum(part, axis=0, keepdims=True)
                at += 1


def row_sums(e_refs, v_ref, acc_ref):
    for row in range(0, acc_ref.shape[0], ROW_HEIGHT):
        acc = [0.0] * (ROW_HEIGHT // 8)
        at = 0
        for e_ref in e_refs:
            for t in tiles(e_ref.shape[1]):
                v = jnp.broadcast_to(v_ref[at : at + 1, :], (8, LANES))
                at += 1
                for k in range(ROW_HEIGHT // 8):
                    acc[k] = acc[k] + e_ref[row + 8 * k : row + 8 * k + 8, t : t + LANES] * v
        for k in range(ROW_HEIGHT // 8):
            acc_ref[row + 8 * k : row + 8 * k + 8, :] = acc[k]


def column_pass(n_parts, log_nt, *refs):
    parts = refs[:n_parts]
    m_ref, a_ref, e0_ref, e1_ref, b0_ref, b1_ref, lam_ref, *f_ref, u_ref = refs[n_parts:]
    rows = a_ref.shape[0]
    pot = log_nt - lse2([ref[...] for ref in parts])
    for ref in f_ref:
        ref[...] = pot
    power = pot + m_ref[...]
    u = jnp.exp2(power)
    to_rows(u, u_ref)
    column_sums((e0_ref, e1_ref), u_ref, lam_ref)
    q = lam_ref[...]
    lam_ref[...] = jnp.log2(q)
    least = jnp.maximum(total_of(u) * 2.0**-106, 2.0**-96)
    fine = every(power > -100.0, (q >= least) & (q < 2.0**120))

    @pl.when(jnp.logical_not(fine))
    def _():
        to_rows(pot, u_ref)
        first = 0
        for b_ref in (b0_ref, b1_ref):

            def block(c, _):
                col = pl.multiple_of(c * LANES, LANES)

                def shifted(i):
                    row = pl.multiple_of(i * LANES, LANES)
                    return scores(a_ref, b_ref, row, LANES, col, LANES) + u_ref[pl.ds(row, LANES), :]

                top = lax.fori_loop(
                    0,
                    rows // LANES,
                    lambda i, best: jnp.maximum(best, jnp.max(shifted(i), axis=0, keepdims=True)),
                    jnp.full((1, LANES), -jnp.inf, f32),
                )
                total = lax.fori_loop(
                    0,
                    rows // LANES,
                    lambda i, acc: acc + jnp.sum(jnp.exp2(shifted(i) - top), axis=0, keepdims=True),
                    jnp.zeros((1, LANES), f32),
                )
                lam_ref[pl.ds(first + c, 1), :] = top + jnp.log2(total)

            lax.fori_loop(0, b_ref.shape[1] // LANES, block, None)
            first += b_ref.shape[1] // LANES


def row_log_sums(change, m_ref, a_ref, e0_ref, e1_ref, b0_ref, b1_ref, rho_ref, v_ref, acc_ref):
    v = jnp.exp2(change)
    v_ref[...] = v
    row_sums((e0_ref, e1_ref), v_ref, acc_ref)
    to_lanes(acc_ref, jnp.sum, rho_ref)
    r = rho_ref[...]
    rho_ref[...] = m_ref[...] + jnp.log2(r)
    least = jnp.maximum(total_of(v) * 2.0**-106, 2.0**-94)
    fine = every(change > -100.0, (r >= least) & (r < 2.0**120))

    @pl.when(jnp.logical_not(fine))
    def _():
        v_ref[...] = change

        def block(i, _):
            row = pl.multiple_of(i * LANES, LANES)

            def over_columns(step, value):
                first = 0
                for b_ref in (b0_ref, b1_ref):

                    def body(c, value):
                        col = pl.multiple_of(c * LANES, LANES)
                        s = scores(a_ref, b_ref, row, LANES, col, LANES) + v_ref[pl.ds(first + c, 1), :]
                        return step(value, s)

                    value = lax.fori_loop(0, b_ref.shape[1] // LANES, body, value)
                    first += b_ref.shape[1] // LANES
                return value

            top = over_columns(
                lambda best, s: jnp.maximum(best, jnp.max(s, axis=1, keepdims=True)),
                jnp.full((LANES, 1), -jnp.inf, f32),
            )
            total = over_columns(
                lambda acc, s: acc + jnp.sum(jnp.exp2(s - top), axis=1, keepdims=True),
                jnp.zeros((LANES, 1), f32),
            )
            value = jnp.broadcast_to(top + jnp.log2(total), (LANES, LANES))
            rho_ref[pl.ds(i, 1), :] = jnp.max(value.T, axis=0, keepdims=True)

        lax.fori_loop(0, a_ref.shape[0] // LANES, block, None)


def row_pass(n_parts, log_ns, *refs):
    parts = refs[:n_parts]
    change = log_ns - lse2([ref[...] for ref in parts])
    row_log_sums(change, *refs[n_parts:])


def marginal_pass(n_parts, log_ns, *refs):
    parts = refs[:n_parts]
    *kept, f_ref, g_ref, _, sum_ref, new_ref, rho_ref, v_ref, acc_ref = refs[n_parts:]
    change = log_ns - lse2([ref[...] for ref in parts])
    new_ref[...] = g_ref[...] + change * (1.0 / KAPPA)
    row_log_sums(change, *kept, rho_ref, v_ref, acc_ref)
    sum_ref[...] = jnp.exp2(f_ref[...] + rho_ref[...])


def others(x, axis, size, steps):
    return [lax.ppermute(x, axis, [(i, i ^ k) for i in range(size)]) for k in steps]


def pool_src(x):
    size = lax.axis_size("src")
    if size == 4:
        return [x] + others(x, "src", size, (1, 2, 3))
    every = lax.all_gather(x, "src", axis=0)
    return [every[k] for k in range(size)]


def pool_tgt(x, join):
    size = lax.axis_size("tgt")
    if size == 8:
        x = join([x] + others(x, "tgt", size, (1,)))
        return [x] + others(x, "tgt", size, (3, 5, 7))
    every = lax.all_gather(x, "tgt", axis=0)
    return [every[k] for k in range(size)]


def body(source_points, target_points, g_init):
    dims, rows = source_points.shape
    cols = target_points.shape[1]
    half = cols // 2
    n_src, n_tgt = lax.axis_size("src"), lax.axis_size("tgt")
    log_nt, log_ns = math.log2(cols * n_tgt), math.log2(rows * n_src)
    depth = 6 * dims + 16
    row_shape, col_shape = (rows // LANES, LANES), (cols // LANES, LANES)
    row, col, square = vmem(row_shape), vmem(col_shape), vmem((rows, LANES))
    e_half, b_half = vmem((rows, half)), vmem((depth, half), bf16)

    def call(kernel, outs, scratch, *args, in_hbm=(), aliases={}):
        return pl.pallas_call(
            kernel,
            out_shape=tuple(outs),
            in_specs=[HBM if k in in_hbm else VMEM for k in range(len(args))],
            out_specs=(VMEM,) * len(outs),
            scratch_shapes=scratch,
            input_output_aliases=aliases,
            compiler_params=PARAMS,
        )(*args)

    split_gather = n_src == 4
    targets = (vmem(target_points.shape),) + (vmem((target_points.shape[0], half)),) * 2
    a, squares, g, g2, *own = call(
        functools.partial(prepare, n_src),
        (vmem((rows, depth), bf16), row, vmem((1, cols)), col) + (targets if split_gather else ()),
        [vmem(source_points.shape), pltpu.SemaphoreType.DMA((6,))],
        *(
            pin(x, pltpu.HBM)
            for x in (source_points, target_points, g_init.reshape(1, cols), g_init.reshape(col_shape))
        ),
        in_hbm=(0, 1, 2, 3),
    )
    if split_gather:
        near = others(target_points, "src", n_src, (1, 2))
        far = [others(pin(x), "src", n_src, (3,))[0] for x in own[1:]]
        blocks = [[own[0], *near, x] for x in far]
    else:
        blocks = [[lax.all_gather(target_points, "src", axis=0, tiled=True)]] * 2
    blocks = [[pin(x) for x in part] for part in blocks]
    a, g = pin(a), pin(g)
    e0, b0, shift, acc = call(
        functools.partial(build_first, len(blocks[0])),
        (e_half, b_half, square, square),
        [],
        a,
        g,
        *blocks[0],
    )
    b0 = pin(b0)
    e0, e1, b1, rho, m = call(
        functools.partial(build_second, len(blocks[1])),
        (e_half, e_half, b_half, row, row),
        [square, square],
        a,
        g,
        *blocks[1],
        pin(e0),
        b0,
        pin(shift),
        pin(acc),
        aliases={2 + len(blocks[1]): 0},
    )
    kept = [pin(m), a, pin(e0), pin(e1), b0, pin(b1)]

    parts = [pin(x) for x in pool_tgt(rho, lse2)]
    (lam,) = call(functools.partial(column_pass, len(parts), log_nt), (col,), [square], *parts, *kept)
    parts = [pin(x) for x in pool_src(lam)]
    (rho,) = call(functools.partial(row_pass, len(parts), log_ns), (row,), [col, square], *parts, *kept)
    parts = [pin(x) for x in pool_tgt(rho, lse2)]
    lam, f = call(functools.partial(column_pass, len(parts), log_nt), (col, row), [square], *parts, *kept)
    parts = [pin(x) for x in pool_src(lam)]
    f_pot = squares + f * (1.0 / KAPPA)
    args = parts + kept + [pin(f), pin(g2), f_pot]
    total, g_pot = call(
        functools.partial(marginal_pass, len(parts), log_ns),
        (row, col),
        [row, col, square],
        *args,
        in_hbm=(len(args) - 1,),
    )
    marginal = sum(pool_tgt(total, sum)) * (1.0 / (cols * n_tgt))
    return f_pot.reshape(rows), g_pot.reshape(cols), marginal.reshape(rows)


def solution(mesh):
    in_specs = (P(None, "src"), P("src", "tgt"), P("tgt"))
    out_specs = (P("src"), P("tgt"), P("src"))
    return jax.shard_map(body, mesh=mesh, in_specs=in_specs, out_specs=out_specs, check_vma=False)
```

```python
import functools
import math

import jax
import jax.numpy as jnp
from jax import lax
from jax.experimental import pallas as pl
from jax.experimental.pallas import tpu as pltpu
from jax.sharding import PartitionSpec as P

epsilon = 0.05
KAPPA = math.log2(math.e) / epsilon
LANES = 128
ROW_BLOCK = 512
COL_BLOCK = 256
COL_WIDTH = 1024

f32 = jnp.float32
bf16 = jnp.bfloat16
VMEM = pl.BlockSpec(memory_space=pltpu.VMEM)
PARAMS = pltpu.CompilerParams(vmem_limit_bytes=16 * 2**20)


HBM = pl.BlockSpec(memory_space=pltpu.HBM)


def vmem(shape, dtype=f32):
    return pltpu.VMEM(shape, dtype)


def pin(x, space=pltpu.VMEM):
    return pltpu.with_memory_space_constraint(x, space)


def split(x):
    first = x.astype(bf16)
    rest = x - first.astype(f32)
    second = rest.astype(bf16)
    third = (rest - second.astype(f32)).astype(bf16)
    return first, second, third


def to_lanes(ref, reduce, out_ref):
    for k in range(out_ref.shape[0]):
        part = ref[k * LANES : (k + 1) * LANES, :].T
        out_ref[k : k + 1, :] = reduce(part, axis=0, keepdims=True)


def to_rows(x, out_ref):
    for k in range(x.shape[0]):
        out_ref[k * LANES : (k + 1) * LANES, :] = jnp.broadcast_to(x[k : k + 1, :], (LANES, LANES)).T


def every(*conditions):
    least = [jnp.min(jnp.where(c, 1.0, 0.0), axis=0, keepdims=True) for c in conditions]
    return jnp.min(functools.reduce(jnp.minimum, least)) > 0.5


def total_of(x):
    return jnp.sum(jnp.sum(x, axis=0, keepdims=True), axis=1, keepdims=True)


def lse2(parts):
    top = functools.reduce(jnp.maximum, parts)
    return top + jnp.log2(sum(jnp.exp2(p - top) for p in parts))


def scores(a_ref, b_ref, row, rows, col, cols):
    return jnp.dot(
        a_ref[pl.ds(row, rows), :], b_ref[:, pl.ds(col, cols)], preferred_element_type=f32
    )


def tiles(width):
    return range(0, width, LANES)


def prepare(n_src, src_ref, t_ref, g_ref, g2_ref, a_ref, square_ref, start_ref, start2_ref, *rest):
    *targets, points_ref, sems = rest
    pairs = [(src_ref, points_ref), (g_ref, start_ref), (g2_ref, start2_ref)]
    if targets:
        own_ref, *halves = targets
        pairs.append((t_ref, own_ref))
        width = halves[0].shape[1]
        pairs += [(t_ref.at[:, pl.ds(k * width, width)], half) for k, half in enumerate(halves)]
    copies = [pltpu.make_async_copy(x, y, sems.at[k]) for k, (x, y) in enumerate(pairs)]
    for copy in copies:
        copy.start()
    for copy in copies:
        copy.wait()
    dims, rows = points_ref.shape
    points = points_ref[...]
    square = jnp.sum(points * points, axis=0, keepdims=True)
    for k in range(rows // LANES):
        square_ref[k : k + 1, :] = square[:, k * LANES : (k + 1) * LANES]
    if n_src == 4:
        me, each = lax.axis_index("src"), dims // n_src
        points = jnp.concatenate(
            [points_ref[pl.ds(pl.multiple_of((me ^ k) * each, each), each), :] for k in range(n_src)],
            axis=0,
        )
    s1, s2, s3 = (x.astype(f32) for x in split(points * (2.0 * KAPPA)))
    last = (lax.broadcasted_iota(jnp.int32, (16, rows), 0) < 3).astype(f32)
    a_ref[...] = jnp.concatenate([s1, s1, s2, s1, s3, s2, last], axis=0).T.astype(bf16)


def fill_right(half, g_ref, blocks, b_ref):
    cols = b_ref.shape[1]
    here = slice(half * cols, (half + 1) * cols)
    points = jnp.concatenate([ref[...] if ref.shape[1] == cols else ref[:, here] for ref in blocks], axis=0)
    dims = points.shape[0]
    t1, t2, t3 = split(points)
    for k, part in enumerate((t1, t2, t1, t3, t1, t2)):
        b_ref[k * dims : (k + 1) * dims, :] = part
    offset = KAPPA * (g_ref[:, here] - jnp.sum(points * points, axis=0, keepdims=True))
    o1, o2, o3 = (x.astype(f32) for x in split(offset))
    fill = jnp.zeros((13, cols), f32)
    b_ref[6 * dims :, :] = jnp.concatenate([o1, o2, o3, fill], axis=0).astype(bf16)


def row_top(a_ref, b_ref, row, col):
    s = scores(a_ref, b_ref, row, ROW_BLOCK, col, COL_BLOCK)
    return s, functools.reduce(jnp.maximum, [s[:, t : t + LANES] for t in tiles(COL_BLOCK)])


def spread(best):
    return jnp.broadcast_to(jnp.max(best, axis=1, keepdims=True), best.shape)


def fill_half(first, a_ref, b_ref, e_ref, shift_ref, start_ref, acc_ref):
    rows, cols = e_ref.shape

    def block(i, _):
        row = pl.multiple_of(i * ROW_BLOCK, ROW_BLOCK)
        here = pl.ds(row, ROW_BLOCK)
        for col in range(0, cols, COL_BLOCK):
            if first and col == 0:
                s, best = row_top(a_ref, b_ref, row, col)
                shift = spread(best)
                shift_ref[here, :] = shift
            else:
                s = scores(a_ref, b_ref, row, ROW_BLOCK, col, COL_BLOCK)
                shift = shift_ref[here, :]
            if col:
                acc = acc_ref[here, :]
            else:
                acc = start_ref[here, :] if start_ref is not None else 0.0
            for t in tiles(COL_BLOCK):
                e = jnp.exp2(s[:, t : t + LANES] - shift)
                e_ref[here, col + t : col + t + LANES] = e
                acc = acc + e
            acc_ref[here, :] = acc

    lax.fori_loop(0, rows // ROW_BLOCK, block, None)


def build_first(n_blocks, *refs):
    a_ref, g_ref = refs[:2]
    blocks = refs[2 : 2 + n_blocks]
    e_ref, b_ref, shift_ref, acc_ref = refs[2 + n_blocks :]
    fill_right(0, g_ref, blocks, b_ref)
    fill_half(True, a_ref, b_ref, e_ref, shift_ref, None, acc_ref)


def build_second(n_blocks, *refs):
    a_ref, g_ref = refs[:2]
    blocks = refs[2 : 2 + n_blocks]
    _, b0_ref, shift_ref, start_ref = refs[2 + n_blocks : 6 + n_blocks]
    e0_ref, e_ref, b_ref, rho_ref, m_ref, acc_ref, exact_ref = refs[6 + n_blocks :]
    to_lanes(shift_ref, jnp.max, m_ref)
    fill_right(1, g_ref, blocks, b_ref)
    fill_half(False, a_ref, b_ref, e_ref, shift_ref, start_ref, acc_ref)

    def finish():
        to_lanes(acc_ref, jnp.sum, rho_ref)
        total = rho_ref[...]
        rho_ref[...] = m_ref[...] + jnp.log2(total)
        return total

    fine = every(finish() < 2.0**100)

    @pl.when(jnp.logical_not(fine))
    def _():
        def block(i, _):
            row = pl.multiple_of(i * ROW_BLOCK, ROW_BLOCK)
            best = jnp.full((ROW_BLOCK, LANES), -jnp.inf, f32)
            for part in (b0_ref, b_ref):
                best = lax.fori_loop(
                    0,
                    part.shape[1] // COL_BLOCK,
                    lambda c, best: jnp.maximum(
                        best, row_top(a_ref, part, row, pl.multiple_of(c * COL_BLOCK, COL_BLOCK))[1]
                    ),
                    best,
                )
            exact_ref[pl.ds(row, ROW_BLOCK), :] = spread(best)

        lax.fori_loop(0, e_ref.shape[0] // ROW_BLOCK, block, None)
        fill_half(False, a_ref, b0_ref, e0_ref, exact_ref, None, acc_ref)
        fill_half(False, a_ref, b_ref, e_ref, exact_ref, acc_ref, acc_ref)
        to_lanes(exact_ref, jnp.max, m_ref)
        finish()


def column_sums(e_refs, u_ref, q_ref):
    at = 0
    for e_ref in e_refs:
        rows, cols = e_ref.shape
        for col in range(0, cols, COL_WIDTH):
            acc = [0.0] * (COL_WIDTH // LANES)
            for row in range(0, rows, 8):
                u = u_ref[row : row + 8, :]
                for k, t in enumerate(tiles(COL_WIDTH)):
                    acc[k] = acc[k] + e_ref[row : row + 8, col + t : col + t + LANES] * u
            for part in acc:
                q_ref[at : at + 1, :] = jnp.sum(part, axis=0, keepdims=True)
                at += 1


def row_sums(e_refs, v_ref, out_ref):
    for k in range(out_ref.shape[0]):
        acc = [0.0] * (LANES // 8)
        at = 0
        for e_ref in e_refs:
            for t in tiles(e_ref.shape[1]):
                v = jnp.broadcast_to(v_ref[at : at + 1, :], (8, LANES))
                at += 1
                for n in range(LANES // 8):
                    row = k * LANES + 8 * n
                    acc[n] = acc[n] + e_ref[row : row + 8, t : t + LANES] * v
        out_ref[k : k + 1, :] = jnp.sum(jnp.concatenate(acc, axis=0).T, axis=0, keepdims=True)


def column_pass(n_parts, log_nt, *refs):
    parts = refs[:n_parts]
    m_ref, a_ref, e0_ref, e1_ref, b0_ref, b1_ref, lam_ref, *f_ref, u_ref = refs[n_parts:]
    rows = a_ref.shape[0]
    pot = log_nt - lse2([ref[...] for ref in parts])
    for ref in f_ref:
        ref[...] = pot
    power = pot + m_ref[...]
    u = jnp.exp2(power)
    least = jnp.maximum(total_of(u) * 2.0**-106, 2.0**-96)
    to_rows(u, u_ref)
    column_sums((e0_ref, e1_ref), u_ref, lam_ref)
    q = lam_ref[...]
    lam_ref[...] = jnp.log2(q)
    fine = every(power > -100.0, (q >= least) & (q < 2.0**120))

    @pl.when(jnp.logical_not(fine))
    def _():
        to_rows(pot, u_ref)
        first = 0
        for b_ref in (b0_ref, b1_ref):

            def block(c, _):
                col = pl.multiple_of(c * LANES, LANES)

                def shifted(i):
                    row = pl.multiple_of(i * LANES, LANES)
                    return scores(a_ref, b_ref, row, LANES, col, LANES) + u_ref[pl.ds(row, LANES), :]

                top = lax.fori_loop(
                    0,
                    rows // LANES,
                    lambda i, best: jnp.maximum(best, jnp.max(shifted(i), axis=0, keepdims=True)),
                    jnp.full((1, LANES), -jnp.inf, f32),
                )
                total = lax.fori_loop(
                    0,
                    rows // LANES,
                    lambda i, acc: acc + jnp.sum(jnp.exp2(shifted(i) - top), axis=0, keepdims=True),
                    jnp.zeros((1, LANES), f32),
                )
                lam_ref[pl.ds(first + c, 1), :] = top + jnp.log2(total)

            lax.fori_loop(0, b_ref.shape[1] // LANES, block, None)
            first += b_ref.shape[1] // LANES


def row_log_sums(change, m_ref, a_ref, e0_ref, e1_ref, b0_ref, b1_ref, rho_ref, v_ref):
    v = jnp.exp2(change)
    v_ref[...] = v
    least = jnp.maximum(total_of(v) * 2.0**-106, 2.0**-94)
    row_sums((e0_ref, e1_ref), v_ref, rho_ref)
    r = rho_ref[...]
    rho_ref[...] = m_ref[...] + jnp.log2(r)
    fine = every(change > -100.0, (r >= least) & (r < 2.0**120))

    @pl.when(jnp.logical_not(fine))
    def _():
        v_ref[...] = change

        def block(i, _):
            row = pl.multiple_of(i * LANES, LANES)

            def over_columns(step, value):
                first = 0
                for b_ref in (b0_ref, b1_ref):

                    def body(c, value):
                        col = pl.multiple_of(c * LANES, LANES)
                        s = scores(a_ref, b_ref, row, LANES, col, LANES) + v_ref[pl.ds(first + c, 1), :]
                        return step(value, s)

                    value = lax.fori_loop(0, b_ref.shape[1] // LANES, body, value)
                    first += b_ref.shape[1] // LANES
                return value

            top = over_columns(
                lambda best, s: jnp.maximum(best, jnp.max(s, axis=1, keepdims=True)),
                jnp.full((LANES, 1), -jnp.inf, f32),
            )
            total = over_columns(
                lambda acc, s: acc + jnp.sum(jnp.exp2(s - top), axis=1, keepdims=True),
                jnp.zeros((LANES, 1), f32),
            )
            value = jnp.broadcast_to(top + jnp.log2(total), (LANES, LANES))
            rho_ref[pl.ds(i, 1), :] = jnp.max(value.T, axis=0, keepdims=True)

        lax.fori_loop(0, a_ref.shape[0] // LANES, block, None)


def row_pass(n_parts, log_ns, *refs):
    parts = refs[:n_parts]
    change = log_ns - lse2([ref[...] for ref in parts])
    row_log_sums(change, *refs[n_parts:])


def marginal_pass(n_parts, log_ns, *refs):
    parts = refs[:n_parts]
    *kept, f_ref, g_ref, _, sum_ref, new_ref, rho_ref, v_ref = refs[n_parts:]
    change = log_ns - lse2([ref[...] for ref in parts])
    new_ref[...] = g_ref[...] + change * (1.0 / KAPPA)
    row_log_sums(change, *kept, rho_ref, v_ref)
    sum_ref[...] = jnp.exp2(f_ref[...] + rho_ref[...])


def others(x, axis, size, steps):
    return [lax.ppermute(x, axis, [(i, i ^ k) for i in range(size)]) for k in steps]


def pool_src(x):
    size = lax.axis_size("src")
    if size == 4:
        return [x] + others(x, "src", size, (1, 2, 3))
    every = lax.all_gather(x, "src", axis=0)
    return [every[k] for k in range(size)]


def pool_tgt(x, join):
    size = lax.axis_size("tgt")
    if size == 8:
        x = join([x] + others(x, "tgt", size, (1,)))
        return [x] + others(x, "tgt", size, (3, 5, 7))
    every = lax.all_gather(x, "tgt", axis=0)
    return [every[k] for k in range(size)]


def body(source_points, target_points, g_init):
    dims, rows = source_points.shape
    cols = target_points.shape[1]
    half = cols // 2
    n_src, n_tgt = lax.axis_size("src"), lax.axis_size("tgt")
    log_nt, log_ns = math.log2(cols * n_tgt), math.log2(rows * n_src)
    depth = 6 * dims + 16
    row_shape, col_shape = (rows // LANES, LANES), (cols // LANES, LANES)
    row, col, square = vmem(row_shape), vmem(col_shape), vmem((rows, LANES))
    e_half, b_half = vmem((rows, half)), vmem((depth, half), bf16)

    def call(kernel, outs, scratch, *args, in_hbm=(), aliases={}):
        return pl.pallas_call(
            kernel,
            out_shape=tuple(outs),
            in_specs=[HBM if k in in_hbm else VMEM for k in range(len(args))],
            out_specs=(VMEM,) * len(outs),
            scratch_shapes=scratch,
            input_output_aliases=aliases,
            compiler_params=PARAMS,
        )(*args)

    split_gather = n_src == 4
    targets = (vmem(target_points.shape),) + (vmem((target_points.shape[0], half)),) * 2
    a, squares, g, g2, *own = call(
        functools.partial(prepare, n_src),
        (vmem((rows, depth), bf16), row, vmem((1, cols)), col) + (targets if split_gather else ()),
        [vmem(source_points.shape), pltpu.SemaphoreType.DMA((6,))],
        *(
            pin(x, pltpu.HBM)
            for x in (source_points, target_points, g_init.reshape(1, cols), g_init.reshape(col_shape))
        ),
        in_hbm=(0, 1, 2, 3),
    )
    if split_gather:
        far, near = others(target_points, "src", n_src, (3, 2))
        first, second = (others(pin(x), "src", n_src, (1,))[0] for x in own[1:])
        blocks = [[own[0], x, near, far] for x in (first, second)]
    else:
        blocks = [[lax.all_gather(target_points, "src", axis=0, tiled=True)]] * 2
    blocks = [[pin(x) for x in part] for part in blocks]
    a, g = pin(a), pin(g)
    e0, b0, shift, acc = call(
        functools.partial(build_first, len(blocks[0])),
        (e_half, b_half, square, square),
        [],
        a,
        g,
        *blocks[0],
    )
    b0 = pin(b0)
    e0, e1, b1, rho, m = call(
        functools.partial(build_second, len(blocks[1])),
        (e_half, e_half, b_half, row, row),
        [square, square],
        a,
        g,
        *blocks[1],
        pin(e0),
        b0,
        pin(shift),
        pin(acc),
        aliases={2 + len(blocks[1]): 0},
    )
    kept = [pin(m), a, pin(e0), pin(e1), b0, pin(b1)]

    parts = [pin(x) for x in pool_tgt(rho, lse2)]
    (lam,) = call(functools.partial(column_pass, len(parts), log_nt), (col,), [square], *parts, *kept)
    parts = [pin(x) for x in pool_src(lam)]
    (rho,) = call(functools.partial(row_pass, len(parts), log_ns), (row,), [col], *parts, *kept)
    parts = [pin(x) for x in pool_tgt(rho, lse2)]
    lam, f = call(functools.partial(column_pass, len(parts), log_nt), (col, row), [square], *parts, *kept)
    parts = [pin(x) for x in pool_src(lam)]
    f_pot = squares + f * (1.0 / KAPPA)
    args = parts + kept + [pin(f), pin(g2), f_pot]
    total, g_pot = call(
        functools.partial(marginal_pass, len(parts), log_ns),
        (row, col),
        [row, col],
        *args,
        in_hbm=(len(args) - 1,),
    )
    marginal = sum(pool_tgt(total, sum)) * (1.0 / (cols * n_tgt))
    return f_pot.reshape(rows), g_pot.reshape(cols), marginal.reshape(rows)


def solution(mesh):
    in_specs = (P(None, "src"), P("src", "tgt"), P("tgt"))
    out_specs = (P("src"), P("tgt"), P("src"))
    return jax.shard_map(body, mesh=mesh, in_specs=in_specs, out_specs=out_specs, check_vma=False)
```

```python
import functools
import math

import jax
import jax.numpy as jnp
from jax import lax
from jax.experimental import pallas as pl
from jax.experimental.pallas import tpu as pltpu
from jax.sharding import PartitionSpec as P

epsilon = 0.05
KAPPA = math.log2(math.e) / epsilon
LANES = 128
ROW_BLOCK = 512
COL_BLOCK = 256
COL_WIDTH = 1024

f32 = jnp.float32
bf16 = jnp.bfloat16
VMEM = pl.BlockSpec(memory_space=pltpu.VMEM)
PARAMS = pltpu.CompilerParams(vmem_limit_bytes=16 * 2**20)


HBM = pl.BlockSpec(memory_space=pltpu.HBM)


def vmem(shape, dtype=f32):
    return pltpu.VMEM(shape, dtype)


def pin(x, space=pltpu.VMEM):
    return pltpu.with_memory_space_constraint(x, space)


def split(x):
    first = x.astype(bf16)
    rest = x - first.astype(f32)
    second = rest.astype(bf16)
    third = (rest - second.astype(f32)).astype(bf16)
    return first, second, third


def to_lanes(ref, reduce, out_ref):
    for k in range(out_ref.shape[0]):
        part = ref[k * LANES : (k + 1) * LANES, :].T
        out_ref[k : k + 1, :] = reduce(part, axis=0, keepdims=True)


def to_rows(x, out_ref):
    for k in range(x.shape[0]):
        out_ref[k * LANES : (k + 1) * LANES, :] = jnp.broadcast_to(x[k : k + 1, :], (LANES, LANES)).T


def every(*conditions):
    least = [jnp.min(jnp.where(c, 1.0, 0.0), axis=0, keepdims=True) for c in conditions]
    return jnp.min(functools.reduce(jnp.minimum, least)) > 0.5


def total_of(x):
    return jnp.sum(jnp.sum(x, axis=0, keepdims=True), axis=1, keepdims=True)


def lse2(parts):
    top = functools.reduce(jnp.maximum, parts)
    return top + jnp.log2(sum(jnp.exp2(p - top) for p in parts))


def scores(a_ref, b_ref, row, rows, col, cols):
    return jnp.dot(
        a_ref[pl.ds(row, rows), :], b_ref[:, pl.ds(col, cols)], preferred_element_type=f32
    )


def tiles(width):
    return range(0, width, LANES)


def prepare(n_src, src_ref, t_ref, g_ref, g2_ref, a_ref, square_ref, start_ref, start2_ref, *rest):
    *targets, points_ref, sems = rest
    pairs = [(src_ref, points_ref), (g_ref, start_ref), (g2_ref, start2_ref)]
    if targets:
        own_ref, *halves = targets
        pairs.append((t_ref, own_ref))
        width = halves[0].shape[1]
        pairs += [(t_ref.at[:, pl.ds(k * width, width)], half) for k, half in enumerate(halves)]
    copies = [pltpu.make_async_copy(x, y, sems.at[k]) for k, (x, y) in enumerate(pairs)]
    for copy in copies:
        copy.start()
    for copy in copies:
        copy.wait()
    dims, rows = points_ref.shape
    points = points_ref[...]
    square = jnp.sum(points * points, axis=0, keepdims=True)
    for k in range(rows // LANES):
        square_ref[k : k + 1, :] = square[:, k * LANES : (k + 1) * LANES]
    if n_src == 4:
        me, each = lax.axis_index("src"), dims // n_src
        points = jnp.concatenate(
            [points_ref[pl.ds(pl.multiple_of((me ^ k) * each, each), each), :] for k in range(n_src)],
            axis=0,
        )
    s1, s2, s3 = (x.astype(f32) for x in split(points * (2.0 * KAPPA)))
    last = (lax.broadcasted_iota(jnp.int32, (16, rows), 0) < 3).astype(f32)
    a_ref[...] = jnp.concatenate([s1, s1, s2, s1, s3, s2, last], axis=0).T.astype(bf16)


def fill_right(half, g_ref, blocks, b_ref):
    cols = b_ref.shape[1]
    here = slice(half * cols, (half + 1) * cols)
    points = jnp.concatenate([ref[...] if ref.shape[1] == cols else ref[:, here] for ref in blocks], axis=0)
    dims = points.shape[0]
    t1, t2, t3 = split(points)
    for k, part in enumerate((t1, t2, t1, t3, t1, t2)):
        b_ref[k * dims : (k + 1) * dims, :] = part
    offset = KAPPA * (g_ref[:, here] - jnp.sum(points * points, axis=0, keepdims=True))
    o1, o2, o3 = (x.astype(f32) for x in split(offset))
    fill = jnp.zeros((13, cols), f32)
    b_ref[6 * dims :, :] = jnp.concatenate([o1, o2, o3, fill], axis=0).astype(bf16)


def row_top(a_ref, b_ref, row, col):
    s = scores(a_ref, b_ref, row, ROW_BLOCK, col, COL_BLOCK)
    return s, functools.reduce(jnp.maximum, [s[:, t : t + LANES] for t in tiles(COL_BLOCK)])


def spread(best):
    return jnp.broadcast_to(jnp.max(best, axis=1, keepdims=True), best.shape)


def fill_half(first, a_ref, b_ref, e_ref, shift_ref, start_ref, acc_ref):
    rows, cols = e_ref.shape

    def block(i, _):
        row = pl.multiple_of(i * ROW_BLOCK, ROW_BLOCK)
        here = pl.ds(row, ROW_BLOCK)
        for col in range(0, cols, COL_BLOCK):
            if first and col == 0:
                s, best = row_top(a_ref, b_ref, row, col)
                shift = spread(best)
                shift_ref[here, :] = shift
            else:
                s = scores(a_ref, b_ref, row, ROW_BLOCK, col, COL_BLOCK)
                shift = shift_ref[here, :]
            if col:
                acc = acc_ref[here, :]
            else:
                acc = start_ref[here, :] if start_ref is not None else 0.0
            for t in tiles(COL_BLOCK):
                e = jnp.exp2(s[:, t : t + LANES] - shift)
                e_ref[here, col + t : col + t + LANES] = e
                acc = acc + e
            acc_ref[here, :] = acc

    lax.fori_loop(0, rows // ROW_BLOCK, block, None)


def build_first(n_blocks, *refs):
    a_ref, g_ref = refs[:2]
    blocks = refs[2 : 2 + n_blocks]
    e_ref, b_ref, shift_ref, acc_ref = refs[2 + n_blocks :]
    fill_right(0, g_ref, blocks, b_ref)
    fill_half(True, a_ref, b_ref, e_ref, shift_ref, None, acc_ref)


def build_second(n_blocks, *refs):
    a_ref, g_ref = refs[:2]
    blocks = refs[2 : 2 + n_blocks]
    _, b0_ref, shift_ref, start_ref = refs[2 + n_blocks : 6 + n_blocks]
    e0_ref, e_ref, b_ref, rho_ref, m_ref, acc_ref, exact_ref = refs[6 + n_blocks :]
    to_lanes(shift_ref, jnp.max, m_ref)
    fill_right(1, g_ref, blocks, b_ref)
    fill_half(False, a_ref, b_ref, e_ref, shift_ref, start_ref, acc_ref)

    def finish():
        to_lanes(acc_ref, jnp.sum, rho_ref)
        total = rho_ref[...]
        rho_ref[...] = m_ref[...] + jnp.log2(total)
        return total

    fine = every(finish() < 2.0**100)

    @pl.when(jnp.logical_not(fine))
    def _():
        def block(i, _):
            row = pl.multiple_of(i * ROW_BLOCK, ROW_BLOCK)
            best = jnp.full((ROW_BLOCK, LANES), -jnp.inf, f32)
            for part in (b0_ref, b_ref):
                best = lax.fori_loop(
                    0,
                    part.shape[1] // COL_BLOCK,
                    lambda c, best: jnp.maximum(
                        best, row_top(a_ref, part, row, pl.multiple_of(c * COL_BLOCK, COL_BLOCK))[1]
                    ),
                    best,
                )
            exact_ref[pl.ds(row, ROW_BLOCK), :] = spread(best)

        lax.fori_loop(0, e_ref.shape[0] // ROW_BLOCK, block, None)
        fill_half(False, a_ref, b0_ref, e0_ref, exact_ref, None, acc_ref)
        fill_half(False, a_ref, b_ref, e_ref, exact_ref, acc_ref, acc_ref)
        to_lanes(exact_ref, jnp.max, m_ref)
        finish()


def column_sums(e_refs, u_ref, q_ref):
    at = 0
    for e_ref in e_refs:
        rows, cols = e_ref.shape
        for col in range(0, cols, COL_WIDTH):
            acc = [0.0] * (COL_WIDTH // LANES)
            for row in range(0, rows, 8):
                u = u_ref[row : row + 8, :]
                for k, t in enumerate(tiles(COL_WIDTH)):
                    acc[k] = acc[k] + e_ref[row : row + 8, col + t : col + t + LANES] * u
            for part in acc:
                q_ref[at : at + 1, :] = jnp.sum(part, axis=0, keepdims=True)
                at += 1


def row_sums(e_refs, v_ref, out_ref):
    for k in range(out_ref.shape[0]):
        acc = [0.0] * (LANES // 8)
        at = 0
        for e_ref in e_refs:
            for t in tiles(e_ref.shape[1]):
                v = jnp.broadcast_to(v_ref[at : at + 1, :], (8, LANES))
                at += 1
                for n in range(LANES // 8):
                    row = k * LANES + 8 * n
                    acc[n] = acc[n] + e_ref[row : row + 8, t : t + LANES] * v
        out_ref[k : k + 1, :] = jnp.sum(jnp.concatenate(acc, axis=0).T, axis=0, keepdims=True)


def column_pass(n_parts, log_nt, *refs):
    parts = refs[:n_parts]
    m_ref, a_ref, e0_ref, e1_ref, b0_ref, b1_ref, lam_ref, *f_ref, u_ref = refs[n_parts:]
    rows = a_ref.shape[0]
    pot = log_nt - lse2([ref[...] for ref in parts])
    for ref in f_ref:
        ref[...] = pot
    power = pot + m_ref[...]
    u = jnp.exp2(power)
    least = jnp.maximum(total_of(u) * 2.0**-106, 2.0**-96)
    to_rows(u, u_ref)
    column_sums((e0_ref, e1_ref), u_ref, lam_ref)
    q = lam_ref[...]
    lam_ref[...] = jnp.log2(q)
    fine = every(power > -100.0, (q >= least) & (q < 2.0**120))

    @pl.when(jnp.logical_not(fine))
    def _():
        to_rows(pot, u_ref)
        first = 0
        for b_ref in (b0_ref, b1_ref):

            def block(c, _):
                col = pl.multiple_of(c * LANES, LANES)

                def shifted(i):
                    row = pl.multiple_of(i * LANES, LANES)
                    return scores(a_ref, b_ref, row, LANES, col, LANES) + u_ref[pl.ds(row, LANES), :]

                top = lax.fori_loop(
                    0,
                    rows // LANES,
                    lambda i, best: jnp.maximum(best, jnp.max(shifted(i), axis=0, keepdims=True)),
                    jnp.full((1, LANES), -jnp.inf, f32),
                )
                total = lax.fori_loop(
                    0,
                    rows // LANES,
                    lambda i, acc: acc + jnp.sum(jnp.exp2(shifted(i) - top), axis=0, keepdims=True),
                    jnp.zeros((1, LANES), f32),
                )
                lam_ref[pl.ds(first + c, 1), :] = top + jnp.log2(total)

            lax.fori_loop(0, b_ref.shape[1] // LANES, block, None)
            first += b_ref.shape[1] // LANES


def row_log_sums(change, m_ref, a_ref, e0_ref, e1_ref, b0_ref, b1_ref, rho_ref, v_ref):
    v = jnp.exp2(change)
    v_ref[...] = v
    least = jnp.maximum(total_of(v) * 2.0**-106, 2.0**-94)
    row_sums((e0_ref, e1_ref), v_ref, rho_ref)
    r = rho_ref[...]
    rho_ref[...] = m_ref[...] + jnp.log2(r)
    fine = every(change > -100.0, (r >= least) & (r < 2.0**120))

    @pl.when(jnp.logical_not(fine))
    def _():
        v_ref[...] = change

        def block(i, _):
            row = pl.multiple_of(i * LANES, LANES)

            def over_columns(step, value):
                first = 0
                for b_ref in (b0_ref, b1_ref):

                    def body(c, value):
                        col = pl.multiple_of(c * LANES, LANES)
                        s = scores(a_ref, b_ref, row, LANES, col, LANES) + v_ref[pl.ds(first + c, 1), :]
                        return step(value, s)

                    value = lax.fori_loop(0, b_ref.shape[1] // LANES, body, value)
                    first += b_ref.shape[1] // LANES
                return value

            top = over_columns(
                lambda best, s: jnp.maximum(best, jnp.max(s, axis=1, keepdims=True)),
                jnp.full((LANES, 1), -jnp.inf, f32),
            )
            total = over_columns(
                lambda acc, s: acc + jnp.sum(jnp.exp2(s - top), axis=1, keepdims=True),
                jnp.zeros((LANES, 1), f32),
            )
            value = jnp.broadcast_to(top + jnp.log2(total), (LANES, LANES))
            rho_ref[pl.ds(i, 1), :] = jnp.max(value.T, axis=0, keepdims=True)

        lax.fori_loop(0, a_ref.shape[0] // LANES, block, None)


def row_pass(n_parts, log_ns, *refs):
    parts = refs[:n_parts]
    change = log_ns - lse2([ref[...] for ref in parts])
    row_log_sums(change, *refs[n_parts:])


def marginal_pass(n_parts, log_ns, *refs):
    parts = refs[:n_parts]
    *kept, f_ref, g_ref, _, sum_ref, new_ref, rho_ref, v_ref = refs[n_parts:]
    change = log_ns - lse2([ref[...] for ref in parts])
    new_ref[...] = g_ref[...] + change * (1.0 / KAPPA)
    row_log_sums(change, *kept, rho_ref, v_ref)
    sum_ref[...] = jnp.exp2(f_ref[...] + rho_ref[...])


def others(x, axis, size, steps):
    return [lax.ppermute(x, axis, [(i, i ^ k) for i in range(size)]) for k in steps]


def pool_src(x):
    size = lax.axis_size("src")
    if size == 4:
        return [x] + others(x, "src", size, (1, 2, 3))
    every = lax.all_gather(x, "src", axis=0)
    return [every[k] for k in range(size)]


def pool_tgt(x, join):
    size = lax.axis_size("tgt")
    if size == 8:
        x = join([x] + others(x, "tgt", size, (1,)))
        return [x] + others(x, "tgt", size, (3, 5, 7))
    every = lax.all_gather(x, "tgt", axis=0)
    return [every[k] for k in range(size)]


def body(source_points, target_points, g_init):
    dims, rows = source_points.shape
    cols = target_points.shape[1]
    half = cols // 2
    n_src, n_tgt = lax.axis_size("src"), lax.axis_size("tgt")
    log_nt, log_ns = math.log2(cols * n_tgt), math.log2(rows * n_src)
    depth = 6 * dims + 16
    row_shape, col_shape = (rows // LANES, LANES), (cols // LANES, LANES)
    row, col, square = vmem(row_shape), vmem(col_shape), vmem((rows, LANES))
    e_half, b_half = vmem((rows, half)), vmem((depth, half), bf16)

    def call(kernel, outs, scratch, *args, in_hbm=(), aliases={}):
        return pl.pallas_call(
            kernel,
            out_shape=tuple(outs),
            in_specs=[HBM if k in in_hbm else VMEM for k in range(len(args))],
            out_specs=(VMEM,) * len(outs),
            scratch_shapes=scratch,
            input_output_aliases=aliases,
            compiler_params=PARAMS,
        )(*args)

    split_gather = n_src == 4
    targets = (vmem(target_points.shape),) + (vmem((target_points.shape[0], half)),) * 2
    a, squares, g, g2, *own = call(
        functools.partial(prepare, n_src),
        (vmem((rows, depth), bf16), row, vmem((1, cols)), col) + (targets if split_gather else ()),
        [vmem(source_points.shape), pltpu.SemaphoreType.DMA((6,))],
        *(
            pin(x, pltpu.HBM)
            for x in (source_points, target_points, g_init.reshape(1, cols), g_init.reshape(col_shape))
        ),
        in_hbm=(0, 1, 2, 3),
    )
    if split_gather:
        near, far = others(target_points, "src", n_src, (2, 3))
        first, second = (others(pin(x), "src", n_src, (1,))[0] for x in own[1:])
        blocks = [[own[0], x, near, far] for x in (first, second)]
    else:
        blocks = [[lax.all_gather(target_points, "src", axis=0, tiled=True)]] * 2
    blocks = [[pin(x) for x in part] for part in blocks]
    a, g = pin(a), pin(g)
    e0, b0, shift, acc = call(
        functools.partial(build_first, len(blocks[0])),
        (e_half, b_half, square, square),
        [],
        a,
        g,
        *blocks[0],
    )
    b0 = pin(b0)
    e0, e1, b1, rho, m = call(
        functools.partial(build_second, len(blocks[1])),
        (e_half, e_half, b_half, row, row),
        [square, square],
        a,
        g,
        *blocks[1],
        pin(e0),
        b0,
        pin(shift),
        pin(acc),
        aliases={2 + len(blocks[1]): 0},
    )
    kept = [pin(m), a, pin(e0), pin(e1), b0, pin(b1)]

    parts = [pin(x) for x in pool_tgt(rho, lse2)]
    (lam,) = call(functools.partial(column_pass, len(parts), log_nt), (col,), [square], *parts, *kept)
    parts = [pin(x) for x in pool_src(lam)]
    (rho,) = call(functools.partial(row_pass, len(parts), log_ns), (row,), [col], *parts, *kept)
    parts = [pin(x) for x in pool_tgt(rho, lse2)]
    lam, f = call(functools.partial(column_pass, len(parts), log_nt), (col, row), [square], *parts, *kept)
    parts = [pin(x) for x in pool_src(lam)]
    f_pot = squares + f * (1.0 / KAPPA)
    args = parts + kept + [pin(f), pin(g2), f_pot]
    total, g_pot = call(
        functools.partial(marginal_pass, len(parts), log_ns),
        (row, col),
        [row, col],
        *args,
        in_hbm=(len(args) - 1,),
    )
    marginal = sum(pool_tgt(total, sum)) * (1.0 / (cols * n_tgt))
    return f_pot.reshape(rows), g_pot.reshape(cols), marginal.reshape(rows)


def solution(mesh):
    in_specs = (P(None, "src"), P("src", "tgt"), P("tgt"))
    out_specs = (P("src"), P("tgt"), P("src"))
    return jax.shard_map(body, mesh=mesh, in_specs=in_specs, out_specs=out_specs, check_vma=False)
```
